512 devices in a mesh: cols: 128 (over z, y, core), rep: 4 (over x).
Axes of the slice: x: 4, y: 4, z: 16, core: 2. Of those that a mesh axis runs over, the one named last changes fastest.
Arguments:
- taxa_states: int32 [32, 65536], P(None, ('cols', 'rep')), may hold values from 0 to 19
- outside: float32 [4, 20, 65536], P(None, None, ('cols', 'rep')), may hold values from 0.001 to 1
- children: int32 [31, 2], replicated, may hold values from 0 to 61, as said below
- branch: float32 [62], replicated, may hold values from 0.02 to 0.08
- root_length: float32 [1], replicated, may hold values from 0.02 to 0.08
- cat_rates: float32 [4], replicated, may hold values from 0.1 to 2.5
- exchange_rates: float32 [20, 20], replicated, may hold values from 0.1 to 1.5
- frequencies: float32 [20], replicated, may hold values from 0.02 to 0.1
- rivals: float32 [99, 65536], P(None, ('cols', 'rep')), may hold values from -120 to -20
- pattern_idx: int32 [131072], P(('cols', 'rep')), may hold values from 0 to 127
- weights: int32 [2048, 131072], P(None, ('cols', 'rep')), may hold values from 0 to 2
Outputs:
- rell_scores: float32 [100, 2048], P(None, ('cols', 'rep'))
- pattern_loglik: float32 [65536], P(('cols', 'rep'))
- root_final: float32 [1], replicated
The draws below stay inside these ranges and needn't reach their ends.
Inputs may be any that keep to these rules, and one draw needn't show every extreme that they name: Row r holds the children of node 32 + r; ids below 32 are taxa; every node but the root, node 62, is a child exactly once, and every child id is below its parent's. `pattern_idx`: local index of the pattern a column shows among the 128 patterns of the column's block of 256 columns.
All inputs are finite; a program needn't handle non-finite values.
Results may differ from the reference program's by a relative error of at most 0.0003.
Values sent between devices are 32-bit elements; how exact they have to be, the bound alone decides.
A program may use at most 64 MiB of HBM per device.

```python
import math
import jax
import jax.numpy as jnp
from jax import lax

STATES = 20
CATS = 4
TERMS = 40
LEAVES = 32
INNER = 31
NODES = 63
EDGES = 62
NEWTON = 3
RIVALS = 99
CAND = 100
REPS = 2048
PAT_DEV = 128
COL_DEV = 256
PATTERNS = 65536
COLUMNS = 131072
N_COLS = 128
N_REP = 4


def column_layout(key):
    layout_key = jax.random.fold_in(key, 29)
    constant_flag = jax.random.randint(jax.random.fold_in(layout_key, 1), (PATTERNS,), 0, 2).astype(jnp.int32)
    constant_state = jax.random.randint(jax.random.fold_in(layout_key, 2), (PATTERNS,), 0, STATES).astype(jnp.int32)
    return (constant_flag, constant_state)


def draw_taxa_states(key, part):
    constant_flag, constant_state = column_layout(key)
    key = jax.random.fold_in(key, 11)
    scattered = jax.random.randint(key, (LEAVES, PATTERNS), 0, STATES).astype(jnp.int32)
    chosen = jnp.where(constant_flag[None, :] == 1, constant_state[None, :], scattered)
    return chosen.astype(jnp.int32)


def draw_outside(key, part):
    key = jax.random.fold_in(key, 13)
    shape = (CATS, STATES, PATTERNS)
    spread = jax.random.uniform(jax.random.fold_in(key, 3), shape, jnp.float32, 0.0, 1.0)
    values = jnp.exp(jnp.log(0.001) * (1.0 - spread))
    return values.astype(jnp.float32)


def draw_children(key, part):
    key = jax.random.fold_in(key, 7)
    pool = jax.random.permutation(jax.random.fold_in(key, 1), LEAVES).astype(jnp.int32)
    pairs = jnp.zeros((INNER, 2), jnp.int32)

    def merge_step(step_index, carry):
        pool, pairs = carry
        alive = LEAVES - step_index
        step_key = jax.random.fold_in(key, 100 + step_index)
        first_pos = jax.random.randint(jax.random.fold_in(step_key, 1), (), 0, alive)
        second_pos = jax.random.randint(jax.random.fold_in(step_key, 2), (), 0, alive - 1)
        second_pos = second_pos + (second_pos >= first_pos).astype(jnp.int32)
        pairs = pairs.at[step_index, 0].set(pool[first_pos])
        pairs = pairs.at[step_index, 1].set(pool[second_pos])
        pool = pool.at[first_pos].set(LEAVES + step_index)
        pool = pool.at[second_pos].set(pool[alive - 1])
        return (pool, pairs)
    pool, pairs = lax.fori_loop(0, INNER, merge_step, (pool, pairs))
    return pairs


def place_ends(entries, rng, smallest, high):
    longest = entries.shape.index(max(entries.shape))
    spots = []
    for shift in (0, 1):
        where = [jax.random.randint(jax.random.fold_in(rng, axis), (), 0, length) for axis, length in enumerate(entries.shape)]
        where[longest] = (where[longest] + shift) % entries.shape[longest]
        spots.append(tuple(where))
    return entries.at[spots[0]].set(smallest).at[spots[1]].set(high)


def shard_levels(key, extent, cuts, smallest, high):
    factor_of, own = 1.0, jax.random.fold_in(key, 6)
    for position, shards_of in cuts:
        heights = jnp.exp(jax.random.uniform(jax.random.fold_in(own, position), (shards_of,), jnp.float32, smallest / len(cuts), high / len(cuts)))
        factor_of = factor_of * jnp.repeat(heights, extent[position] // shards_of).reshape([-1 if axis == position else 1 for axis in range(len(extent))])
    return factor_of


def setup_inputs(seed: int = 0) -> dict:
    arg_keys = jax.random.split(jax.random.key(seed), 12)
    return {
        "taxa_states": draw_taxa_states(jax.random.fold_in(arg_keys[11], 71), 0),
        "outside": draw_outside(jax.random.fold_in(arg_keys[11], 71), 0),
        "children": draw_children(jax.random.fold_in(arg_keys[11], 71), 0),
        "branch": jnp.clip(jnp.exp(jax.random.uniform(arg_keys[3], (EDGES,), jnp.float32, math.log(0.02), math.log(0.08))), 0.02, 0.08),
        "root_length": jnp.clip(jnp.exp(jax.random.uniform(arg_keys[4], (1,), jnp.float32, math.log(0.02), math.log(0.08))), 0.02, 0.08),
        "cat_rates": jnp.clip(jnp.exp(jax.random.uniform(arg_keys[5], (CATS,), jnp.float32, math.log(0.1), math.log(2.5))), 0.1, 2.5),
        "exchange_rates": jnp.clip(jax.random.uniform(arg_keys[6], (STATES, STATES), jnp.float32, 0.1, 1.5), 0.1, 1.5),
        "frequencies": jnp.clip(jax.random.uniform(arg_keys[7], (STATES,), jnp.float32, 0.02, 0.1), 0.02, 0.1),
        "rivals": jnp.clip(-120.0 + 100.0 * jax.random.uniform(arg_keys[8], (RIVALS, PATTERNS), jnp.float32) ** shard_levels(arg_keys[8], (RIVALS, PATTERNS), ((1, 512),), -0.2, 0.2), -120.0, -20.0),
        "pattern_idx": place_ends(jax.random.randint(arg_keys[9], (COLUMNS,), 0, PAT_DEV), jax.random.fold_in(arg_keys[9], 1), 0, PAT_DEV - 1).astype(jnp.int32),
        "weights": place_ends(jax.random.randint(arg_keys[10], (REPS, COLUMNS), 0, 3), jax.random.fold_in(arg_keys[10], 1), 0, 2).astype(jnp.int32),
    }


MU_RATE = 4.0
LENGTH_CAP = 2.0
highest = lax.Precision.HIGHEST


def rate_powers(exchange_rates, frequencies):
    states = exchange_rates.shape[0]
    identity = jnp.eye(states, dtype=jnp.float32)
    symmetric = 0.5 * (exchange_rates + exchange_rates.T)
    offdiag = symmetric * frequencies[None, :] * (1.0 - identity)
    generator = offdiag - jnp.diag(jnp.sum(offdiag, axis=1))
    stepping = identity + generator / MU_RATE

    def advance(current, unused):
        following = jnp.dot(current, stepping, precision=highest)
        return following, current

    unused_last, powers = lax.scan(advance, identity, None, length=TERMS)
    return powers


def term_weights(scaled):
    orders = jnp.arange(TERMS).astype(jnp.float32)
    logged = -scaled[..., None] + orders * jnp.log(scaled)[..., None] - lax.lgamma(orders + 1.0)
    return jnp.exp(logged)


def edge_transitions(branch, cat_rates, powers):
    mixing = term_weights(MU_RATE * branch[:, None] * cat_rates[None, :])
    return jnp.einsum("eck,kij->ecij", mixing, powers, precision=highest)


def prune_block(taxa_block, outside_block, children, transitions, powers, frequencies):
    pattern_count = taxa_block.shape[1]
    onehot = (taxa_block[:, None, :] == jnp.arange(STATES)[None, :, None]).astype(jnp.float32)
    partials = jnp.zeros((NODES, CATS, STATES, pattern_count), jnp.float32)
    partials = partials.at[:LEAVES].set(jnp.broadcast_to(onehot[:, None], (LEAVES, CATS, STATES, pattern_count)))
    log_scales = jnp.zeros((NODES, pattern_count), jnp.float32)

    def merge_step(step_index, carry):
        partials, log_scales = carry
        first_child = children[step_index, 0]
        second_child = children[step_index, 1]
        left_msg = jnp.einsum("cij,cjs->cis", transitions[first_child], partials[first_child], precision=highest)
        right_msg = jnp.einsum("cij,cjs->cis", transitions[second_child], partials[second_child], precision=highest)
        product = left_msg * right_msg
        largest = jnp.max(product, axis=(0, 1))
        node_id = LEAVES + step_index
        partials = partials.at[node_id].set(product / largest)
        log_scales = log_scales.at[node_id].set(log_scales[first_child] + log_scales[second_child] + jnp.log(largest))
        return partials, log_scales

    partials, log_scales = lax.fori_loop(0, INNER, merge_step, (partials, log_scales))
    root_partial = partials[NODES - 1]
    weighted_outside = frequencies[None, :, None] * outside_block
    lifted = jnp.einsum("kij,cjs->ckis", powers, root_partial, precision=highest)
    moment_basis = jnp.einsum("cis,ckis->cks", weighted_outside, lifted, precision=highest)
    return moment_basis, log_scales[NODES - 1]


def derivatives(moment_basis, length, cat_rates):
    speeds = MU_RATE * cat_rates
    mixing = term_weights(speeds * length)
    zeros_one = jnp.zeros((CATS, 1), mixing.dtype)
    shifted_once = jnp.concatenate([zeros_one, mixing[:, :-1]], axis=1)
    shifted_twice = jnp.concatenate([zeros_one, shifted_once[:, :-1]], axis=1)
    slope_terms = speeds[:, None] * (shifted_once - mixing)
    bend_terms = (speeds * speeds)[:, None] * (shifted_twice - 2.0 * shifted_once + mixing)
    stacked = jnp.stack([mixing, slope_terms, bend_terms])
    return 0.25 * jnp.einsum("nck,cks->ns", stacked, moment_basis, precision=highest)


def local_sums(values, counts):
    ratio_terms = values[1] / values[0]
    first_sum = jnp.sum(counts * ratio_terms)
    second_sum = jnp.sum(counts * (values[2] / values[0] - ratio_terms * ratio_terms))
    return first_sum, second_sum


def newton_update(length, first_sum, second_sum):
    proposal = length - first_sum / jnp.minimum(second_sum, -1.0)
    return jnp.clip(proposal, 0.25 * length, LENGTH_CAP)


def reference(taxa_states, outside, children, branch, root_length, cat_rates, exchange_rates, frequencies, rivals, pattern_idx, weights):
    blocks = N_COLS * N_REP
    powers = rate_powers(exchange_rates, frequencies)
    transitions = edge_transitions(branch, cat_rates, powers)
    taxa_blocks = taxa_states.reshape(LEAVES, blocks, PAT_DEV).transpose(1, 0, 2)
    outside_blocks = outside.reshape(CATS, STATES, blocks, PAT_DEV).transpose(2, 0, 1, 3)

    def one_block(pieces):
        return prune_block(pieces[0], pieces[1], children, transitions, powers, frequencies)

    basis_blocks, scale_blocks = lax.map(one_block, (taxa_blocks, outside_blocks))
    moment_basis = basis_blocks.transpose(1, 2, 0, 3).reshape(CATS, TERMS, PATTERNS)
    root_scale = scale_blocks.reshape(PATTERNS)
    offsets = (jnp.arange(COLUMNS) // COL_DEV).astype(jnp.int32) * PAT_DEV
    global_idx = (pattern_idx + offsets).astype(jnp.int32)
    counts = jax.ops.segment_sum(jnp.ones((COLUMNS,), jnp.float32), global_idx, num_segments=PATTERNS)
    length = root_length[0]
    for newton_step in range(NEWTON):
        values = derivatives(moment_basis, length, cat_rates)
        first_sum, second_sum = local_sums(values, counts)
        length = newton_update(length, first_sum, second_sum)
    final_values = derivatives(moment_basis, length, cat_rates)
    pattern_loglik = jnp.log(final_values[0]) + root_scale
    scored = jnp.concatenate([pattern_loglik[None, :], rivals], axis=0)

    def add_block(running, block_index):
        column_start = block_index * COL_DEV
        block_weights = lax.dynamic_slice_in_dim(weights, column_start, COL_DEV, 1).astype(jnp.float32)
        block_patterns = lax.dynamic_slice_in_dim(pattern_idx, column_start, COL_DEV, 0)
        tallies = jax.ops.segment_sum(block_weights.T, block_patterns, num_segments=PAT_DEV)
        block_scores = lax.dynamic_slice_in_dim(scored, block_index * PAT_DEV, PAT_DEV, 1)
        return running + jnp.dot(block_scores, tallies, precision=highest), None

    running, unused = lax.scan(add_block, jnp.zeros((CAND, REPS), jnp.float32), jnp.arange(blocks).astype(jnp.int32))
    rell_scores = running / COLUMNS
    return rell_scores, pattern_loglik, length[None]
```

```python
import functools
import math

import jax
import jax.numpy as jnp
import numpy as np
from jax import lax
from jax.experimental import pallas as pl
from jax.experimental.pallas import tpu as pltpu
from jax.sharding import PartitionSpec as P

STATES = 20
CATS = 4
TERMS = 40
LEAVES = 32
INNER = 31
EDGES = 62
NEWTON = 3
RIVALS = 99
CAND = 100
MU_RATE = 4.0
LENGTH_CAP = 2.0
CORES = 2
BLOCK = CATS * STATES
PAD = 24
f32 = jnp.float32
bf16 = jnp.bfloat16
MESH = pl.DeviceIdType.MESH
highest = lax.Precision.HIGHEST


def layout_of(mesh):
    cols, chips_x = mesh.shape["cols"], mesh.shape["rep"]
    chips_y = 4 if cols >= 128 else 2
    return dict(z=cols // (CORES * chips_y), y=chips_y, c=CORES, x=chips_x)


def position(dims):
    cols = lax.axis_index("cols")
    return dict(
        z=cols // (dims["y"] * dims["c"]),
        y=(cols // dims["c"]) % dims["y"],
        c=cols % dims["c"],
        x=lax.axis_index("rep"),
    )


def device_of(dims, at):
    return ((at["z"] * dims["y"] + at["y"]) * dims["c"] + at["c"], at["x"])


def group_size(dims, axes):
    return math.prod(dims[a] for a in axes)


def group_index(dims, axes, at):
    index = 0
    for a in axes:
        index = index * dims[a] + at[a]
    return index


def group_member(dims, axes, at, index):
    member = dict(at)
    for a in reversed(axes):
        member[a] = index % dims[a]
        index = index // dims[a]
    return member


def tree_sum(values):
    while len(values) > 1:
        paired = [values[i] + values[i + 1] for i in range(0, len(values) - 1, 2)]
        if len(values) % 2:
            paired.append(values[-1])
        values = paired
    return values[0]


def split_high(value):
    return value.astype(bf16).astype(f32)


def iota(shape, axis):
    return lax.broadcasted_iota(jnp.int32, shape, axis)


def pick(index, entries, base):
    chosen = base
    for number, entry in enumerate(entries):
        chosen = jnp.where(index == number, entry, chosen)
    return chosen


PLANE = ("y", "x")
COLUMN = ("z", "c")
LINE = ("z",)


def kernel(
    dims,
    lg_lane,
    lg_row,
    taxa,
    outside,
    children,
    branch,
    root_length,
    rates,
    exchange,
    freqs,
    pattern,
    rivals_hbm,
    weights_hbm,
    out_scores,
    out_loglik,
    out_root,
    w_int,
    riv,
    w_b,
    onehot_b,
    square,
    pow_a,
    pow_b,
    x_col,
    t_a,
    t_b,
    msg,
    largest_rows,
    prod_s,
    root_s,
    lhs_s,
    wo_s,
    m_s,
    score_s,
    pair_r,
    rs_a,
    rs_r1,
    rs_b,
    rs_r2,
    val_a,
    val_b,
    ar_a,
    ar_b,
    row_v,
    row_r1,
    row_u,
    row_r2,
    load_sem,
    ar_send,
    ar_recv,
    rs_send,
    rs_recv,
    row_send,
    row_recv,
):
    at = position(dims)
    reps = score_s.shape[0] * CORES * score_s.shape[2] * 8
    lanes_z = reps // dims["z"]

    barrier = pltpu.get_barrier_semaphore()
    greeted = 0
    for axes in (PLANE, COLUMN):
        size, mine = group_size(dims, axes), group_index(dims, axes, at)
        for step in range(1, size):
            peer = group_member(dims, axes, at, (mine + step) % size)
            pl.semaphore_signal(barrier, inc=1, device_id=device_of(dims, peer), device_id_type=MESH)
            greeted += 1

    weights_copy = pltpu.make_async_copy(weights_hbm, w_int, load_sem.at[0])
    rivals_copy = pltpu.make_async_copy(rivals_hbm, riv, load_sem.at[1])
    weights_copy.start()
    rivals_copy.start()

    square[...] = jnp.zeros_like(square)
    square[0:STATES, 0:STATES] = exchange[...]
    full = square[...]
    symmetric = (0.5 * (full + full.T))[0:PAD]
    row24, lane24 = iota((PAD, 128), 0), iota((PAD, 128), 1)
    freq_row = pick(iota((1, 128), 1), [freqs[j] for j in range(STATES)], jnp.zeros((1, 128), f32))
    off = jnp.where(row24 == lane24, 0.0, symmetric * freq_row)
    away = jnp.sum(off, axis=1, keepdims=True)
    inside = (row24 == lane24) & (row24 < STATES)
    eye = jnp.where(inside, 1.0, jnp.zeros((PAD, 128), f32))
    stepping = eye + (off - jnp.where(inside, away, 0.0)) / MU_RATE

    def spread(block):
        twice = block + pltpu.roll(block, 20, 1)
        four = twice + pltpu.roll(twice, 40, 1)
        low = jnp.where(lane24 < 80, four, pltpu.roll(four, 80, 1))
        return low, pltpu.roll(low, 120, 1)

    for k, block in enumerate((eye, stepping)):
        low, high = spread(block)
        pow_a[k * PAD : (k + 1) * PAD, :] = low
        pow_b[k * PAD : (k + 1) * PAD, :] = high
    reach = 1
    while reach < TERMS:
        count = min(reach + 1, TERMS - reach)
        right = jnp.concatenate(
            [pow_a[reach * PAD : (reach + 1) * PAD, :], pow_b[reach * PAD : (reach + 1) * PAD, :]], axis=1
        )
        right = jnp.concatenate([right, jnp.zeros((128 - PAD, 256), f32)], axis=0)
        product = jnp.dot(pow_a[0 : count * PAD, :], right, precision=highest, preferred_element_type=f32)
        pow_a[reach * PAD : (reach + count) * PAD, :] = product[:, 0:128]
        pow_b[reach * PAD : (reach + count) * PAD, :] = product[:, 128:256]
        reach *= 2

    row8 = iota((8, 128), 0)
    speed = [MU_RATE * rates[c] for c in range(CATS)]
    speed8 = pick(row8 % CATS, speed, jnp.zeros((8, 128), f32))
    for pair in range(EDGES // 2):
        x_col[pair * 8 : pair * 8 + 8, :] = speed8 * jnp.where(row8 < CATS, branch[2 * pair], branch[2 * pair + 1])
    x_col[EDGES * CATS :, :] = jnp.ones((8, 128), f32)
    scaled = x_col[...]
    lane1 = iota((1, 128), 1)
    part = (lane1 >= 40).astype(jnp.int32) + (lane1 >= 80).astype(jnp.int32) + (lane1 >= 120).astype(jnp.int32)
    order = (lane1 - 40 * part).astype(f32)
    mixing = jnp.exp(-scaled + order * jnp.log(scaled) - lg_lane[...])
    mixing_high = split_high(mixing)
    mixing = jnp.where(part == 2, mixing - mixing_high, jnp.where(part == 3, 0.0, mixing_high))
    mixing = mixing.astype(bf16)

    lane256 = iota((1, 256), 1)
    copy256 = (lane256 >= 80).astype(jnp.int32) + (lane256 >= 160).astype(jnp.int32) + (lane256 >= 240).astype(jnp.int32)
    within = lane256 - 80 * copy256
    cat256 = (within >= 20).astype(jnp.int32) + (within >= 40).astype(jnp.int32) + (within >= 60).astype(jnp.int32)
    cat256 = jnp.where(copy256 == 3, -1, cat256)
    keep = (iota((256, 1), 0) % CATS) == cat256
    lane128 = iota((1, 128), 1)
    lhs_part = (lane128 >= 40).astype(jnp.int32) + (lane128 >= 80).astype(jnp.int32) + (lane128 >= 100).astype(jnp.int32)
    lhs_used = (lane128 < 20) | ((lane128 >= 40) & (lane128 < 60)) | ((lane128 >= 80) & (lane128 < 100))
    for i in range(STATES):
        base_a = pow_a[pl.ds(i, TERMS, stride=PAD), :]
        base_b = pow_b[pl.ds(i, TERMS, stride=PAD), :]
        base = jnp.concatenate([base_a, base_b], axis=1)
        base_high = split_high(base)
        right = jnp.concatenate([base_high, base - base_high, base_high, jnp.zeros((8, 256), f32)], axis=0)
        made = jnp.dot(mixing, right.astype(bf16), preferred_element_type=f32)
        made_high = split_high(made)
        made = jnp.where(keep, jnp.where(copy256 == 1, made - made_high, made_high), 0.0)
        t_a[pl.ds(i, 256, stride=STATES), :] = made[:, 0:128]
        t_b[pl.ds(i, 256, stride=STATES), :] = made[:, 128:256]
        a_high = base_high[:, 0:128]
        lhs_s[i * TERMS : (i + 1) * TERMS, :] = jnp.where(
            lhs_used, jnp.where(lhs_part == 1, base_a - a_high, a_high), 0.0
        )

    state80 = iota((BLOCK, 128), 0)
    state80 = state80 - 20 * (
        (state80 >= 20).astype(jnp.int32) + (state80 >= 40).astype(jnp.int32) + (state80 >= 60).astype(jnp.int32)
    )

    def leaf_step(n, carry):
        hot = jnp.where(state80 == taxa[pl.ds(n, 1), :], 1.0, jnp.zeros((BLOCK, 128), f32)).astype(bf16)
        start = pl.multiple_of(n * BLOCK, 16)
        left = jnp.concatenate([t_a[pl.ds(start, BLOCK), :], t_b[pl.ds(start, BLOCK), 0:32]], axis=1)
        right = jnp.concatenate([hot, hot], axis=0)
        msg[n] = jnp.dot(left.astype(bf16), right, preferred_element_type=f32)
        return carry

    lax.fori_loop(0, LEAVES, leaf_step, 0, unroll=4)

    largest_rows[...] = jnp.ones_like(largest_rows)

    def merged(r):
        return msg[children[r, 0]] * msg[children[r, 1]]

    def inner_step(r, carry):
        product = merged(r)
        largest = jnp.max(product, axis=0, keepdims=True)
        largest_rows[pl.ds(r, 1), :] = largest
        high = product.astype(bf16)
        low = (product - high.astype(f32)).astype(bf16)
        right = jnp.concatenate([high, high, low, jnp.zeros((16, 128), bf16)], axis=0)
        start = pl.multiple_of((LEAVES + r) * BLOCK, 16)
        left = jnp.concatenate([t_a[pl.ds(start, BLOCK), :], t_b[pl.ds(start, BLOCK), :]], axis=1)
        moved = jnp.dot(left.astype(bf16), right, preferred_element_type=f32)
        msg[LEAVES + r] = moved * (1.0 / largest)
        return carry

    lax.fori_loop(0, INNER - 1, inner_step, 0)
    product = merged(INNER - 1)
    largest = jnp.max(product, axis=0, keepdims=True)
    largest_rows[INNER - 1 : INNER, :] = largest
    prod_s[...] = product * (1.0 / largest)
    root_scale = jnp.sum(jnp.log(largest_rows[...]), axis=0, keepdims=True)

    root_s[...] = jnp.zeros_like(root_s)
    for c in range(CATS):
        piece = prod_s[c * STATES : (c + 1) * STATES, :]
        piece_high = split_high(piece)
        root_s[0:STATES, c * 128 : (c + 1) * 128] = piece_high
        root_s[40 : 40 + STATES, c * 128 : (c + 1) * 128] = piece_high
        root_s[80 : 80 + STATES, c * 128 : (c + 1) * 128] = piece - piece_high
    freq_col = pick(iota((STATES, 128), 0), [freqs[j] for j in range(STATES)], jnp.zeros((STATES, 128), f32))
    for c in range(CATS):
        wo_s[c] = freq_col * outside[c]
    root_b = root_s[...].astype(bf16)
    lhs_b = lhs_s[...].astype(bf16)
    lifted = jnp.dot(lhs_b, root_b, preferred_element_type=f32)
    m_s[...] = jnp.zeros_like(m_s)
    for c in range(CATS):
        basis = jnp.zeros((TERMS, 128), f32)
        for i in range(STATES):
            basis = basis + lifted[i * TERMS : (i + 1) * TERMS, c * 128 : (c + 1) * 128] * wo_s[c, i : i + 1, :]
        m_s[c, 0:TERMS, :] = basis
    order_row = iota((TERMS, 128), 0).astype(f32)
    lg_rows = lg_row[...]
    basis0, basis1, basis2 = [], [], []
    for c in range(CATS):
        here, next1, next2 = m_s[c, 0:TERMS, :], m_s[c, 1 : TERMS + 1, :], m_s[c, 2 : TERMS + 2, :]
        basis0.append(here)
        basis1.append(speed[c] * (next1 - here))
        basis2.append((speed[c] * speed[c]) * (next2 - 2.0 * next1 + here))

    hot = jnp.where(iota((128, 256), 0) == pattern[...], 1.0, jnp.zeros((128, 256), f32)).astype(bf16)
    onehot_b[...] = hot
    counts = lax.dot_general(
        jnp.ones((16, 256), bf16), hot, (((1,), (1,)), ((), ())), preferred_element_type=f32
    )[0:1]

    def series(length, bases):
        totals = [jnp.zeros((TERMS, 128), f32) for _ in bases]
        for c in range(CATS):
            x = speed[c] * length
            w = jnp.exp(-x + order_row * jnp.log(x) - lg_rows)
            totals = [total + w * basis[c] for total, basis in zip(totals, bases)]
        return [0.25 * jnp.sum(total, axis=0, keepdims=True) for total in totals]

    def local_sums(length):
        value, slope, bend = series(length, (basis0, basis1, basis2))
        ratio = slope / value
        return counts * ratio, counts * (bend / value - ratio * ratio)

    def send_group(axes, source, target, send, recv):
        size, mine = group_size(dims, axes), group_index(dims, axes, at)
        for step in range(1, size):
            slot = (mine + step) % size
            peer = group_member(dims, axes, at, slot)
            pltpu.make_async_remote_copy(
                src_ref=source(slot),
                dst_ref=target.at[mine],
                send_sem=send,
                recv_sem=recv,
                device_id=device_of(dims, peer),
                device_id_type=MESH,
            ).start()

    def wait_group(target, sem):
        several = target.at[pl.ds(0, target.shape[0] - 1)]
        pltpu.make_async_copy(several, several, sem).wait()

    plane_mine, column_mine = group_index(dims, PLANE, at), group_index(dims, COLUMN, at)
    line_mine = at["z"]

    def rivals_scores():
        weights_copy.wait()
        rivals_copy.wait()
        w_b[...] = w_int[...].astype(f32).astype(bf16)
        rows = jnp.concatenate([riv[...], jnp.zeros((128 - RIVALS, 128), f32)], axis=0)
        high = rows.astype(bf16)
        low = (rows - high.astype(f32)).astype(bf16)
        both = jnp.concatenate([high, low], axis=0)
        gathered = jnp.dot(both, onehot_b[...], preferred_element_type=f32).astype(bf16)
        chunk = min(256, reps)
        for begin in range(0, reps, chunk):
            scores = lax.dot_general(
                w_b[begin : begin + chunk, :], gathered, (((1,), (1,)), ((), ())), preferred_element_type=f32
            )
            scores = scores[:, 0:128] + scores[:, 128:256]
            per = CORES * score_s.shape[2] * 8
            score_s[begin // per : (begin + chunk) // per] = scores.reshape(
                (chunk // per,) + score_s.shape[1:]
            )
        pltpu.make_async_remote_copy(
            src_ref=score_s.at[:, 1 - at["c"]],
            dst_ref=pair_r,
            send_sem=rs_send.at[0],
            recv_sem=rs_recv.at[0],
            device_id=device_of(dims, dict(at, c=1 - at["c"])),
            device_id_type=MESH,
        ).start()

    def rivals_plane():
        pltpu.make_async_copy(pair_r, pair_r, rs_recv.at[0]).wait()
        first_half = iota((1, 1, 8, 128), 2) < 4
        tiles = score_s.shape[2]
        chips_y = dims["y"]

        def pair_step(zp, carry):
            even_at = pl.ds(2 * zp * chips_y, chips_y)
            odd_at = pl.ds((2 * zp + 1) * chips_y, chips_y)
            even = score_s[even_at, at["c"]] + pair_r[even_at]
            odd = score_s[odd_at, at["c"]] + pair_r[odd_at]
            even_turned, odd_turned = pltpu.roll(even, 4, 2), pltpu.roll(odd, 4, 2)
            lower = jnp.where(first_half, even, odd_turned)
            upper = jnp.where(first_half, even_turned, odd)
            for t in range(tiles):
                rs_a[:, 2 * t, zp] = lower[:, t]
                rs_a[:, 2 * t + 1, zp] = upper[:, t]
            return carry

        lax.fori_loop(0, dims["z"] // 2, pair_step, 0)
        rs_r1[plane_mine] = rs_a[at["y"], at["x"]]
        send_group(
            PLANE,
            lambda slot: rs_a.at[slot // dims["x"], slot % dims["x"]],
            rs_r1,
            rs_send.at[1],
            rs_recv.at[1],
        )

    def rivals_line():
        wait_group(rs_r1, rs_recv.at[1])
        rs_b[...] = tree_sum([rs_r1[k] for k in range(rs_r1.shape[0])])
        rs_r2[line_mine] = rs_b[at["z"] // 2]
        send_group(LINE, lambda slot: rs_b.at[slot // 2], rs_r2, rs_send.at[2], rs_recv.at[2])

    columns_total = float(pattern.shape[1] * dims["z"] * dims["y"] * dims["c"] * dims["x"])

    def rivals_finish():
        wait_group(rs_r2, rs_recv.at[2])
        total = tree_sum([rs_r2[k] for k in range(rs_r2.shape[0])]) / columns_total
        square[...] = jnp.zeros_like(square)
        square[0:8, :] = total
        turned = square[...].T
        turned = jnp.where(at["z"] % 2 == 0, turned, pltpu.roll(turned, 124, 1))
        out_scores[1:CAND, :] = turned[0:RIVALS, 0:4]

    pl.semaphore_wait(barrier, greeted)
    length = jnp.full((1, 128), root_length[0], f32)
    hidden = [(rivals_scores, rivals_plane), (rivals_line, rivals_finish), (None, None)]
    for step in range(NEWTON):
        first, second = local_sums(length)
        val_a[step, 0:1, :] = first
        val_a[step, 1:2, :] = second
        ar_a[step, plane_mine] = val_a[step]
        send_group(PLANE, lambda slot: val_a.at[step], ar_a.at[step], ar_send.at[step, 0], ar_recv.at[step, 0])
        if hidden[step][0] is not None:
            hidden[step][0]()
        wait_group(ar_a.at[step], ar_recv.at[step, 0])
        val_b[step] = tree_sum([ar_a[step, k] for k in range(ar_a.shape[1])])
        ar_b[step, column_mine] = val_b[step]
        send_group(COLUMN, lambda slot: val_b.at[step], ar_b.at[step], ar_send.at[step, 1], ar_recv.at[step, 1])
        if hidden[step][1] is not None:
            hidden[step][1]()
        wait_group(ar_b.at[step], ar_recv.at[step, 1])
        sums = tree_sum([ar_b[step, k] for k in range(ar_b.shape[1])])
        sums = jnp.sum(sums, axis=1, keepdims=True)
        proposal = length - sums[0:1] / jnp.minimum(sums[1:2], -1.0)
        length = jnp.clip(proposal, 0.25 * length, LENGTH_CAP)
    out_root[...] = length

    (value,) = series(length, (basis0,))
    loglik = jnp.log(value) + root_scale
    out_loglik[...] = loglik
    high = split_high(loglik)
    middle = split_high(loglik - high)
    low = loglik - high - middle
    row16 = iota((16, 128), 0)
    parts = pick(row16, [high, middle, low], jnp.zeros((16, 128), f32)).astype(bf16)
    gathered = jnp.dot(parts, onehot_b[...], preferred_element_type=f32).astype(bf16)
    own = lax.dot_general(gathered, w_b[...], (((1,), (1,)), ((), ())), preferred_element_type=f32)
    own = jnp.sum(own, axis=0, keepdims=True)
    if lanes_z != 128:
        row_v[...] = jnp.zeros_like(row_v)
    for z in range(dims["z"]):
        row_v[z, :, 0:lanes_z] = own[:, z * lanes_z : (z + 1) * lanes_z]
    row_r1[column_mine] = row_v[at["z"]]
    send_group(COLUMN, lambda slot: row_v.at[slot // dims["c"]], row_r1, row_send.at[0], row_recv.at[0])
    wait_group(row_r1, row_recv.at[0])
    row_u[...] = tree_sum([row_r1[k] for k in range(row_r1.shape[0])])
    row_r2[plane_mine] = row_u[...]
    send_group(PLANE, lambda slot: row_u, row_r2, row_send.at[1], row_recv.at[1])
    wait_group(row_r2, row_recv.at[1])
    total = tree_sum([row_r2[k] for k in range(row_r2.shape[0])]) / columns_total
    shift = ((at["y"] * dims["c"] + at["c"]) * dims["x"] + at["x"]) * 4
    total = pltpu.roll(jnp.broadcast_to(total, (8, 128)), 128 - shift, 1)
    out_scores[0:1, :] = total[0:1, 0:4]

    for step in range(NEWTON):
        wait_group(ar_a.at[step], ar_send.at[step, 0])
        wait_group(ar_b.at[step], ar_send.at[step, 1])
    pltpu.make_async_copy(pair_r, pair_r, rs_send.at[0]).wait()
    wait_group(rs_r1, rs_send.at[1])
    wait_group(rs_r2, rs_send.at[2])
    wait_group(row_r1, row_send.at[0])
    wait_group(row_r2, row_send.at[1])


def on_device(
    dims,
    taxa_states,
    outside,
    children,
    branch,
    root_length,
    cat_rates,
    exchange_rates,
    frequencies,
    rivals,
    pattern_idx,
    weights,
):
    reps, columns = weights.shape
    patterns = taxa_states.shape[1]
    z, y, c, x = (dims[a] for a in ("z", "y", "c", "x"))
    tiles = x // 2
    plane, column = group_size(dims, PLANE), group_size(dims, COLUMN)
    log_factorials = np.array([math.lgamma(k + 1.0) for k in range(TERMS)], np.float32)
    lg_lane = np.zeros((1, 128), np.float32)
    for part in range(3):
        lg_lane[0, part * TERMS : (part + 1) * TERMS] = log_factorials
    lg_row = np.broadcast_to(log_factorials[:, None], (TERMS, 128))
    vmem = pl.BlockSpec(memory_space=pltpu.VMEM)
    smem = pl.BlockSpec(memory_space=pltpu.SMEM)
    hbm = pl.BlockSpec(memory_space=pl.ANY)
    scores, loglik, root = pl.pallas_call(
        functools.partial(kernel, dims),
        out_shape=(
            jax.ShapeDtypeStruct((CAND, 4), f32),
            jax.ShapeDtypeStruct((1, patterns), f32),
            jax.ShapeDtypeStruct((1, 128), f32),
        ),
        in_specs=[vmem, vmem, vmem, vmem, smem, smem, smem, smem, vmem, smem, vmem, hbm, hbm],
        out_specs=(vmem, vmem, vmem),
        scratch_shapes=[
            pltpu.VMEM((reps, columns), jnp.int32),
            pltpu.VMEM((RIVALS, 128), f32),
            pltpu.VMEM((reps, columns), bf16),
            pltpu.VMEM((128, columns), bf16),
            pltpu.VMEM((128, 128), f32),
            pltpu.VMEM((TERMS * PAD, 128), f32),
            pltpu.VMEM((TERMS * PAD, 128), f32),
            pltpu.VMEM((256, 128), f32),
            pltpu.VMEM((256 * STATES, 128), f32),
            pltpu.VMEM((256 * STATES, 128), f32),
            pltpu.VMEM((EDGES, BLOCK, 128), f32),
            pltpu.VMEM((32, 128), f32),
            pltpu.VMEM((BLOCK, 128), f32),
            pltpu.VMEM((128, CATS * 128), f32),
            pltpu.VMEM((STATES * TERMS, 128), f32),
            pltpu.VMEM((CATS, STATES, 128), f32),
            pltpu.VMEM((CATS, TERMS + 8, 128), f32),
            pltpu.VMEM((z * y, c, tiles, 8, 128), f32),
            pltpu.VMEM((z * y, tiles, 8, 128), f32),
            pltpu.VMEM((y, x, z // 2, 8, 128), f32),
            pltpu.VMEM((plane, z // 2, 8, 128), f32),
            pltpu.VMEM((z // 2, 8, 128), f32),
            pltpu.VMEM((z, 8, 128), f32),
            pltpu.VMEM((NEWTON, 2, 128), f32),
            pltpu.VMEM((NEWTON, 2, 128), f32),
            pltpu.VMEM((NEWTON, plane, 2, 128), f32),
            pltpu.VMEM((NEWTON, column, 2, 128), f32),
            pltpu.VMEM((z, 1, 128), f32),
            pltpu.VMEM((column, 1, 128), f32),
            pltpu.VMEM((1, 128), f32),
            pltpu.VMEM((plane, 1, 128), f32),
            pltpu.SemaphoreType.DMA((2,)),
            pltpu.SemaphoreType.DMA((NEWTON, 2)),
            pltpu.SemaphoreType.DMA((NEWTON, 2)),
            pltpu.SemaphoreType.DMA((3,)),
            pltpu.SemaphoreType.DMA((3,)),
            pltpu.SemaphoreType.DMA((2,)),
            pltpu.SemaphoreType.DMA((2,)),
        ],
        compiler_params=pltpu.CompilerParams(
            collective_id=0, has_side_effects=True, vmem_limit_bytes=48 * 1024 * 1024
        ),
    )(
        lg_lane,
        lg_row,
        taxa_states,
        outside,
        children,
        branch,
        root_length,
        cat_rates,
        exchange_rates,
        frequencies,
        pattern_idx.reshape(1, columns),
        rivals,
        weights,
    )
    return scores, loglik.reshape(patterns), root[0, 0:1]


def solution(mesh):
    placed = (
        P(None, ("cols", "rep")),
        P(None, None, ("cols", "rep")),
        P(),
        P(),
        P(),
        P(),
        P(),
        P(),
        P(None, ("cols", "rep")),
        P(("cols", "rep")),
        P(None, ("cols", "rep")),
    )
    return jax.shard_map(
        functools.partial(on_device, layout_of(mesh)),
        mesh=mesh,
        in_specs=placed,
        out_specs=(P(None, ("cols", "rep")), P(("cols", "rep")), P()),
        check_vma=False,
    )
```

```python
import functools
import math

import jax
import jax.numpy as jnp
from jax import lax
from jax.experimental import pallas as pl
from jax.experimental.pallas import tpu as pltpu
from jax.sharding import PartitionSpec as P

STATES = 20
CATS = 4
TERMS = 40
LEAVES = 32
INNER = 31
EDGES = 62
NEWTON = 3
RIVALS = 99
CAND = 100
MU_RATE = 4.0
LENGTH_CAP = 2.0
CORES = 2
BLOCK = CATS * STATES
PAD = 24
f32 = jnp.float32
bf16 = jnp.bfloat16
LOG_FACTORIALS = [math.lgamma(k + 1.0) for k in range(TERMS)]
MESH = pl.DeviceIdType.MESH
LEAF_UNROLL = 32
DIRECT_SLACK = 2
LEVELS = DIRECT_SLACK + 1
INNER_UNROLL = 1


def layout_of(mesh):
    cols, chips_x = mesh.shape["cols"], mesh.shape["rep"]
    chips_y = 4 if cols >= 128 else 2
    return dict(z=cols // (CORES * chips_y), y=chips_y, c=CORES, x=chips_x)


def position(dims):
    cols = lax.axis_index("cols")
    return dict(
        z=cols // (dims["y"] * dims["c"]),
        y=(cols // dims["c"]) % dims["y"],
        c=cols % dims["c"],
        x=lax.axis_index("rep"),
    )


def device_of(dims, at):
    return ((at["z"] * dims["y"] + at["y"]) * dims["c"] + at["c"], at["x"])


def group_size(dims, axes):
    return math.prod(dims[a] for a in axes)


def group_index(dims, axes, at):
    index = 0
    for a in axes:
        index = index * dims[a] + at[a]
    return index


def group_member(dims, axes, at, index):
    member = dict(at)
    for a in reversed(axes):
        member[a] = index % dims[a]
        index = index // dims[a]
    return member


def tree_sum(values):
    while len(values) > 1:
        paired = [values[i] + values[i + 1] for i in range(0, len(values) - 1, 2)]
        if len(values) % 2:
            paired.append(values[-1])
        values = paired
    return values[0]


def split_high(value):
    return value.astype(bf16).astype(f32)


def iota(shape, axis):
    return lax.broadcasted_iota(jnp.int32, shape, axis)


def pick(index, entries, base):
    chosen = base
    for number, entry in enumerate(entries):
        chosen = jnp.where(index == number, entry, chosen)
    return chosen


def ring(step, size):
    return min(step, size - step)


def routes(dims):
    plane = sorted(
        ((ring(dy, dims["y"]) + ring(dx, dims["x"]), dy, dx) for dy in range(dims["y"]) for dx in range(dims["x"]))
    )
    column = sorted(((ring(dz, dims["z"]), dz, flip) for dz in range(dims["z"]) for flip in range(dims["c"])))
    most = plane[-1][0] + column[-1][0] - DIRECT_SLACK
    direct = [
        (dz, flip, dy, dx)
        for far, dz, flip in reversed(column)
        for wide, dy, dx in reversed(plane)
        if far > 0 and wide > 0 and far + wide > most
    ]

    def reach(here, limits):
        return max(other for other in limits if here == 0 or other == 0 or here + other <= most)

    wides, fars = sorted({p[0] for p in plane}), sorted({p[0] for p in column})
    column_needs = {far: reach(far, wides) for far in fars}
    plane_needs = {wide: reach(wide, fars) for wide in wides}
    return plane, column, direct, column_needs, plane_needs


PLANE = ("y", "x")
COLUMN = ("z", "c")
LINE = ("z",)


def kernel(
    dims,
    taxa_hbm,
    outside_hbm,
    children_hbm,
    branch_hbm,
    root_length_hbm,
    rates_hbm,
    exchange_hbm,
    freqs_hbm,
    pattern_hbm,
    rivals_hbm,
    weights_hbm,
    out_scores,
    out_loglik,
    out_root,
    taxa,
    outside,
    children,
    branch,
    root_length,
    rates,
    exchange,
    freqs,
    pattern,
    w_int,
    riv,
    w_b,
    onehot_b,
    square,
    powers,
    x_col,
    t_leaf,
    t_high,
    t_low,
    msg,
    largest_rows,
    prod_s,
    root_s,
    lhs_s,
    wo_s,
    m_s,
    score_s,
    pair_r,
    rs_a,
    rs_r1,
    rs_b,
    rs_r2,
    val_a,
    val_b,
    ar_a,
    ar_b,
    ar_d,
    row_v,
    row_r1,
    row_u,
    row_r2,
    row_d,
    root_a,
    root_b,
    root_c,
    root_m,
    load_sem,
    ar_send,
    ar_recv,
    rs_send,
    rs_recv,
    row_send,
    row_recv,
    root_send,
    root_recv,
):
    at = position(dims)
    reps = score_s.shape[0] * CORES * score_s.shape[2] * 8
    lanes_z = reps // dims["z"]

    loads = {}
    for number, (name, source, target) in enumerate(
        (
            ("exchange", exchange_hbm, exchange),
            ("freqs", freqs_hbm, freqs),
            ("rates", rates_hbm, rates),
            ("branch", branch_hbm, branch),
            ("taxa", taxa_hbm, taxa),
            ("children", children_hbm, children),
            ("root", root_length_hbm, root_length),
            ("outside", outside_hbm, outside),
            ("pattern", pattern_hbm, pattern),
            ("weights", weights_hbm, w_int),
            ("rivals", rivals_hbm, riv),
        )
    ):
        loads[name] = pltpu.make_async_copy(source, target, load_sem.at[number])
        loads[name].start()

    plane_offsets, column_offsets, direct_offsets, column_needs, plane_needs = routes(dims)

    def peer_at(dz=0, flip=0, dy=0, dx=0):
        core = at["c"] if flip == 0 else 1 - at["c"]
        there = dict(z=(at["z"] + dz) % dims["z"], c=core, y=(at["y"] + dy) % dims["y"], x=(at["x"] + dx) % dims["x"])
        return there, device_of(dims, there)

    barrier = pltpu.get_barrier_semaphore()
    greeted = [peer_at(dz, flip)[1] for _, dz, flip in column_offsets[1:]]
    greeted += [peer_at(dy=dy, dx=dx)[1] for _, dy, dx in plane_offsets[1:]]
    greeted += [peer_at(*offset)[1] for offset in direct_offsets]
    for device in greeted:
        pl.semaphore_signal(barrier, inc=1, device_id=device, device_id_type=MESH)

    square[...] = jnp.zeros_like(square)
    loads["exchange"].wait()
    loads["freqs"].wait()
    square[0:STATES, 0:STATES] = exchange[...]
    full = square[...]
    symmetric = (0.5 * (full + full.T))[0:PAD]
    row24, lane24 = iota((PAD, 128), 0), iota((PAD, 128), 1)
    freq_row = pick(iota((1, 128), 1), [freqs[j] for j in range(STATES)], jnp.zeros((1, 128), f32))
    off = jnp.where(row24 == lane24, 0.0, symmetric * freq_row)
    away = jnp.sum(off, axis=1, keepdims=True)
    inside = (row24 == lane24) & (row24 < STATES)
    eye = jnp.where(inside, 1.0, jnp.zeros((PAD, 128), f32))
    stepping = eye + (off - jnp.where(inside, away, 0.0)) / MU_RATE

    def spread(block):
        twice = block + pltpu.roll(block, 20, 1)
        four = twice + pltpu.roll(twice, 40, 1)
        return jnp.where(lane24 < 80, four, pltpu.roll(four, 80, 1))

    def three_parts(value):
        high = split_high(value)
        middle = split_high(value - high)
        return high, middle, value - high - middle

    powers[0:PAD, :] = spread(eye)
    powers[PAD : 2 * PAD, :] = spread(stepping)
    lane1 = iota((1, 128), 1)
    reach = 1
    while reach < TERMS:
        count = min(reach + 1, TERMS - reach)
        high, middle, low = three_parts(powers[reach * PAD : (reach + 1) * PAD, :])
        for slot, piece in enumerate((high, middle, low, high, middle, high)):
            square[slot * STATES : (slot + 1) * STATES, :] = piece[0:STATES]
        square[120:128, :] = jnp.zeros((8, 128), f32)
        high, middle, low = three_parts(powers[0 : count * PAD, :])
        left = jnp.where(lane1 < 60, high, jnp.where(lane1 < 100, middle, jnp.where(lane1 < 120, low, 0.0)))
        powers[reach * PAD : (reach + count) * PAD, :] = jnp.dot(
            left.astype(bf16), square[...].astype(bf16), preferred_element_type=f32
        )
        reach *= 2

    loads["rates"].wait()
    loads["branch"].wait()
    row8 = iota((8, 128), 0)
    speed = [MU_RATE * rates[c] for c in range(CATS)]
    speed8 = pick(row8 % CATS, speed, jnp.zeros((8, 128), f32))
    for pair in range(EDGES // 2):
        x_col[pair * 8 : pair * 8 + 8, :] = speed8 * jnp.where(row8 < CATS, branch[2 * pair], branch[2 * pair + 1])
    x_col[EDGES * CATS :, :] = jnp.ones((8, 128), f32)
    scaled = x_col[...]
    part = (lane1 >= 40).astype(jnp.int32) + (lane1 >= 80).astype(jnp.int32) + (lane1 >= 120).astype(jnp.int32)
    order = lane1 - 40 * part
    lg_lane = pick(order, LOG_FACTORIALS, jnp.zeros((1, 128), f32))
    order = order.astype(f32)
    mixing = jnp.exp(-scaled + order * jnp.log(scaled) - lg_lane)
    mixing_high = split_high(mixing)
    mixing = jnp.where(part == 2, mixing - mixing_high, jnp.where(part == 3, 0.0, mixing_high))
    mixing = mixing.astype(bf16)

    cat128 = (lane1 >= 20).astype(jnp.int32) + (lane1 >= 40).astype(jnp.int32) + (lane1 >= 60).astype(jnp.int32)
    cat128 = jnp.where(lane1 < BLOCK, cat128, -1)
    keep = (iota((128, 1), 0) % CATS) == cat128
    lhs_part = (lane1 >= 40).astype(jnp.int32)
    lhs_part = lhs_part + (lane1 >= 80).astype(jnp.int32)
    lhs_used = (lane1 < 20) | ((lane1 >= 40) & (lane1 < 60)) | ((lane1 >= 80) & (lane1 < 100))
    for i in range(STATES):
        base = powers[pl.ds(i, TERMS, stride=PAD), :]
        base_high = split_high(base)
        base_low = base - base_high
        right = jnp.concatenate([base_high, base_low, base_high, jnp.zeros((8, 128), f32)], axis=0)
        made = jnp.dot(mixing, right.astype(bf16), preferred_element_type=f32)
        made_high = split_high(made)
        made_low = made - made_high
        t_leaf[pl.ds(i, 128, stride=STATES), :] = jnp.where(
            lane1 < 20, made_high[0:128], jnp.where(lane1 < 40, made_low[0:128], 0.0)
        )
        t_high[pl.ds(i, 128, stride=STATES), :] = jnp.where(keep, made_high[128:256], 0.0)
        t_low[pl.ds(i, 128, stride=STATES), :] = jnp.where(keep, made_low[128:256], 0.0)
        lhs_s[i * TERMS : (i + 1) * TERMS, :] = jnp.where(
            lhs_used, jnp.where(lhs_part == 1, base_low, base_high), 0.0
        )

    state48 = iota((48, 128), 0)
    state48 = jnp.where(state48 < 20, state48, jnp.where(state48 < 40, state48 - 20, -1))
    loads["taxa"].wait()

    def leaf_step(n, carry):
        hot = jnp.where(state48 == taxa[pl.ds(n, 1), :], 1.0, jnp.zeros((48, 128), f32)).astype(bf16)
        start = pl.multiple_of(n * BLOCK, 16)
        left = t_leaf[pl.ds(start, BLOCK), 0:48]
        msg[n] = jnp.dot(left.astype(bf16), hot, preferred_element_type=f32)
        return carry

    lax.fori_loop(0, LEAVES, leaf_step, 0, unroll=LEAF_UNROLL)

    largest_rows[...] = jnp.ones_like(largest_rows)
    loads["children"].wait()

    def merged(r):
        return msg[children[0, r]] * msg[children[1, r]]

    def inner_step(r, carry):
        product = merged(r)
        largest = jnp.max(product, axis=0, keepdims=True)
        largest_rows[pl.ds(r, 1), :] = largest
        high = product.astype(bf16)
        low = (product - high.astype(f32)).astype(bf16)
        start = pl.multiple_of(r * BLOCK, 16)
        left_high = t_high[pl.ds(start, BLOCK), 0:BLOCK].astype(bf16)
        left_low = t_low[pl.ds(start, BLOCK), 0:BLOCK].astype(bf16)
        both = jnp.dot(jnp.concatenate([left_high, left_low], axis=0), high, preferred_element_type=f32)
        rest = jnp.dot(left_high, low, preferred_element_type=f32)
        moved = both[0:BLOCK] + both[BLOCK:] + rest
        msg[LEAVES + r] = moved * (1.0 / largest)
        return carry

    lax.fori_loop(0, INNER - 1, inner_step, 0, unroll=INNER_UNROLL)
    product = merged(INNER - 1)
    largest = jnp.max(product, axis=0, keepdims=True)
    largest_rows[INNER - 1 : INNER, :] = largest
    prod_s[...] = product * (1.0 / largest)
    root_scale = jnp.sum(jnp.log(largest_rows[...]), axis=0, keepdims=True)

    root_s[...] = jnp.zeros_like(root_s)
    for c in range(CATS):
        piece = prod_s[c * STATES : (c + 1) * STATES, :]
        piece_high = split_high(piece)
        root_s[0:STATES, c * 128 : (c + 1) * 128] = piece_high
        root_s[40 : 40 + STATES, c * 128 : (c + 1) * 128] = piece_high
        root_s[80 : 80 + STATES, c * 128 : (c + 1) * 128] = piece - piece_high
    loads["outside"].wait()
    for i in range(STATES):
        wo_s[i] = freqs[i] * outside[i]
    root_parts = root_s[...].astype(bf16)
    lhs_b = lhs_s[...].astype(bf16)
    lifted = jnp.dot(lhs_b, root_parts, preferred_element_type=f32)
    m_s[...] = jnp.zeros_like(m_s)
    for c in range(CATS):
        basis = jnp.zeros((TERMS, 128), f32)
        for i in range(STATES):
            basis = basis + lifted[i * TERMS : (i + 1) * TERMS, c * 128 : (c + 1) * 128] * wo_s[i, c : c + 1, :]
        m_s[c, 0:TERMS, :] = basis
    order_row = iota((TERMS, 128), 0).astype(f32)
    lg_rows = jnp.concatenate(
        [pick(row8, LOG_FACTORIALS[k : k + 8], jnp.zeros((8, 128), f32)) for k in range(0, TERMS, 8)], axis=0
    )
    basis0, basis1, basis2 = [], [], []
    for c in range(CATS):
        here, next1, next2 = m_s[c, 0:TERMS, :], m_s[c, 1 : TERMS + 1, :], m_s[c, 2 : TERMS + 2, :]
        basis0.append(here)
        basis1.append(speed[c] * (next1 - here))
        basis2.append((speed[c] * speed[c]) * (next2 - 2.0 * next1 + here))

    loads["pattern"].wait()
    loads["root"].wait()
    hot = jnp.where(iota((128, 256), 0) == pattern[...], 1.0, jnp.zeros((128, 256), f32)).astype(bf16)
    onehot_b[...] = hot
    counts = lax.dot_general(
        jnp.ones((16, 256), bf16), hot, (((1,), (1,)), ((), ())), preferred_element_type=f32
    )[0:1]

    def series(length, bases):
        totals = [jnp.zeros((TERMS, 128), f32) for _ in bases]
        for c in range(CATS):
            x = speed[c] * length
            w = jnp.exp(-x + order_row * jnp.log(x) - lg_rows)
            totals = [total + w * basis[c] for total, basis in zip(totals, bases)]
        return [0.25 * jnp.sum(total, axis=0, keepdims=True) for total in totals]

    def local_sums(length):
        value, slope, bend = series(length, (basis0, basis1, basis2))
        ratio = slope / value
        return counts * ratio, counts * (bend / value - ratio * ratio)

    def send_group(axes, source, target, send, recv):
        size, mine = group_size(dims, axes), group_index(dims, axes, at)
        for step in range(1, size):
            slot = (mine + step) % size
            peer = group_member(dims, axes, at, slot)
            pltpu.make_async_remote_copy(
                src_ref=source(slot),
                dst_ref=target.at[mine],
                send_sem=send,
                recv_sem=recv,
                device_id=device_of(dims, peer),
                device_id_type=MESH,
            ).start()

    def wait_group(target, sem):
        several = target.at[pl.ds(0, target.shape[0] - 1)]
        pltpu.make_async_copy(several, several, sem).wait()

    def send(source, target, send_sem, recv_sem, device):
        pltpu.make_async_remote_copy(
            src_ref=source,
            dst_ref=target,
            send_sem=send_sem,
            recv_sem=recv_sem,
            device_id=device,
            device_id_type=MESH,
        ).start()

    def wait_for(target, sem):
        pltpu.make_async_copy(target, target, sem).wait()

    def relay(offsets, heard, heard_sems, own, needs, forward):
        total, begin = own, 1
        for level, reach in enumerate(sorted(set(needs.values()))):
            end = sum(1 for offset in offsets if offset[0] <= reach)
            if end > begin:
                wait_for(heard.at[pl.ds(begin, end - begin)], heard_sems.at[level])
                total = total + tree_sum([heard[k] for k in range(begin, end)])
                begin = end
            forward(level, [distance for distance, needed in needs.items() if needed == reach], total)
        return total

    def level_of(distance, needs):
        return min(level for level, reach in enumerate(sorted(set(needs.values()))) if distance <= reach)

    def all_sum(step, row, meanwhile, meanwhile_later):
        sems_s, sems_r = ar_send.at[step], ar_recv.at[step]
        val_a[step] = row
        for slot, (wide, dy, dx) in reversed(list(enumerate(plane_offsets))[1:]):
            level = level_of(wide, column_needs)
            send(val_a.at[step], ar_a.at[step, slot], sems_s.at[0], sems_r.at[level], peer_at(dy=dy, dx=dx)[1])
        for slot, offset in enumerate(direct_offsets):
            send(val_a.at[step], ar_d.at[step, slot], sems_s.at[1], sems_r.at[LEVELS], peer_at(*offset)[1])
        meanwhile()

        def forward(level, distances, total):
            val_b[step, level] = total
            for slot, (far, dz, flip) in reversed(list(enumerate(column_offsets))[1:]):
                if far in distances:
                    send(
                        val_b.at[step, level],
                        ar_b.at[step, slot],
                        sems_s.at[2],
                        sems_r.at[LEVELS + 1],
                        peer_at(dz, flip)[1],
                    )

        total = relay(plane_offsets, ar_a.at[step], sems_r, row, column_needs, forward)
        meanwhile_later()
        wait_for(ar_d.at[step], sems_r.at[LEVELS])
        total = total + tree_sum([ar_d[step, k] for k in range(len(direct_offsets))])
        others = len(column_offsets) - 1
        wait_for(ar_b.at[step, pl.ds(1, others)], sems_r.at[LEVELS + 1])
        return total + tree_sum([ar_b[step, k] for k in range(1, others + 1)])

    plane_mine = group_index(dims, PLANE, at)
    line_mine = at["z"]

    def rivals_scores():
        loads["weights"].wait()
        loads["rivals"].wait()
        w_b[...] = w_int[...].astype(f32).astype(bf16)
        rows = jnp.concatenate([riv[...], jnp.zeros((128 - RIVALS, 128), f32)], axis=0)
        high = rows.astype(bf16)
        low = (rows - high.astype(f32)).astype(bf16)
        both = jnp.concatenate([high, low], axis=0)
        gathered = jnp.dot(both, onehot_b[...], preferred_element_type=f32).astype(bf16)
        chunk = min(256, reps)
        for begin in range(0, reps, chunk):
            scores = lax.dot_general(
                w_b[begin : begin + chunk, :], gathered, (((1,), (1,)), ((), ())), preferred_element_type=f32
            )
            scores = scores[:, 0:128] + scores[:, 128:256]
            per = CORES * score_s.shape[2] * 8
            score_s[begin // per : (begin + chunk) // per] = scores.reshape(
                (chunk // per,) + score_s.shape[1:]
            )
        pltpu.make_async_remote_copy(
            src_ref=score_s.at[:, 1 - at["c"]],
            dst_ref=pair_r,
            send_sem=rs_send.at[0],
            recv_sem=rs_recv.at[0],
            device_id=device_of(dims, dict(at, c=1 - at["c"])),
            device_id_type=MESH,
        ).start()

    def rivals_plane():
        pltpu.make_async_copy(pair_r, pair_r, rs_recv.at[0]).wait()
        first_half = iota((1, 1, 8, 128), 2) < 4
        tiles = score_s.shape[2]
        chips_y = dims["y"]

        def pair_step(zp, carry):
            even_at = pl.ds(2 * zp * chips_y, chips_y)
            odd_at = pl.ds((2 * zp + 1) * chips_y, chips_y)
            even = score_s[even_at, at["c"]] + pair_r[even_at]
            odd = score_s[odd_at, at["c"]] + pair_r[odd_at]
            even_turned, odd_turned = pltpu.roll(even, 4, 2), pltpu.roll(odd, 4, 2)
            lower = jnp.where(first_half, even, odd_turned)
            upper = jnp.where(first_half, even_turned, odd)
            for t in range(tiles):
                rs_a[:, 2 * t, zp] = lower[:, t]
                rs_a[:, 2 * t + 1, zp] = upper[:, t]
            return carry

        lax.fori_loop(0, dims["z"] // 2, pair_step, 0)
        rs_r1[plane_mine] = rs_a[at["y"], at["x"]]
        send_group(
            PLANE,
            lambda slot: rs_a.at[slot // dims["x"], slot % dims["x"]],
            rs_r1,
            rs_send.at[1],
            rs_recv.at[1],
        )

    def rivals_line():
        wait_group(rs_r1, rs_recv.at[1])
        rs_b[...] = tree_sum([rs_r1[k] for k in range(rs_r1.shape[0])])
        rs_r2[line_mine] = rs_b[at["z"] // 2]
        send_group(LINE, lambda slot: rs_b.at[slot // 2], rs_r2, rs_send.at[2], rs_recv.at[2])

    columns_total = float(pattern.shape[1] * dims["z"] * dims["y"] * dims["c"] * dims["x"])

    def rivals_finish():
        wait_group(rs_r2, rs_recv.at[2])
        total = tree_sum([rs_r2[k] for k in range(rs_r2.shape[0])]) / columns_total
        total = jnp.where(at["z"] % 2 == 0, total, pltpu.roll(total, 4, 0))
        out_scores[...] = pltpu.roll(total, 1, 1)[0:4, 0:CAND]

    pl.semaphore_wait(barrier, len(greeted))
    length = jnp.full((1, 128), root_length[0, 0], f32)

    def nothing():
        return None

    hidden = [(rivals_scores, rivals_plane), (rivals_line, rivals_finish), (nothing, nothing)]
    left_half = lane1 < 64
    for step in range(NEWTON):
        first, second = local_sums(length)
        folded = jnp.where(left_half, first + pltpu.roll(first, 64, 1), second + pltpu.roll(second, 64, 1))
        sums = all_sum(step, folded, *hidden[step])
        first = jnp.sum(jnp.where(left_half, sums, 0.0), axis=1, keepdims=True)
        second = jnp.sum(jnp.where(left_half, 0.0, sums), axis=1, keepdims=True)
        proposal = length - first / jnp.minimum(second, -1.0)
        length = jnp.clip(proposal, 0.25 * length, LENGTH_CAP)

    root_a[...] = length
    head_column = (at["z"] == 0) & (at["c"] == 0)
    head_plane = (at["y"] == 0) & (at["x"] == 0)

    @pl.when(head_column)
    def _():
        root_m[...] = length
        for _, dz, flip in column_offsets[1:]:
            send(root_a, root_b, root_send.at[0], root_recv.at[0], peer_at(dz, flip)[1])


    (value,) = series(length, (basis0,))
    loglik = jnp.log(value) + root_scale
    out_loglik[...] = loglik
    high = split_high(loglik)
    middle = split_high(loglik - high)
    low = loglik - high - middle
    row16 = iota((16, 128), 0)
    parts = pick(row16, [high, middle, low], jnp.zeros((16, 128), f32)).astype(bf16)
    gathered = jnp.dot(parts, onehot_b[...], preferred_element_type=f32).astype(bf16)
    own = lax.dot_general(gathered, w_b[...], (((1,), (1,)), ((), ())), preferred_element_type=f32)
    own = jnp.sum(own, axis=0, keepdims=True)
    if lanes_z != 128:
        row_v[...] = jnp.zeros_like(row_v)
    for z in range(dims["z"]):
        row_v[z, :, 0:lanes_z] = own[:, z * lanes_z : (z + 1) * lanes_z]
    for slot, (far, dz, flip) in reversed(list(enumerate(column_offsets))[1:]):
        there, device = peer_at(dz, flip)
        level = level_of(far, plane_needs)
        send(row_v.at[there["z"]], row_r1.at[slot], row_send.at[0], row_recv.at[level], device)
    for slot, offset in enumerate(direct_offsets):
        there, device = peer_at(*offset)
        send(row_v.at[there["z"]], row_d.at[slot], row_send.at[1], row_recv.at[LEVELS], device)

    def forward_row(level, distances, total):
        row_u[level] = total
        for slot, (wide, dy, dx) in reversed(list(enumerate(plane_offsets))[1:]):
            if wide in distances:
                device = peer_at(dy=dy, dx=dx)[1]
                send(row_u.at[level], row_r2.at[slot], row_send.at[2], row_recv.at[LEVELS + 1], device)

    total = relay(column_offsets, row_r1, row_recv, row_v[at["z"]], plane_needs, forward_row)

    @pl.when(jnp.logical_not(head_column))
    def _():
        wait_for(root_b, root_recv.at[0])
        root_m[...] = root_b[...]

    @pl.when(head_plane)
    def _():
        for _, dy, dx in plane_offsets[1:]:
            send(root_m, root_c, root_send.at[1], root_recv.at[1], peer_at(dy=dy, dx=dx)[1])

    wait_for(row_d, row_recv.at[LEVELS])
    total = total + tree_sum([row_d[k] for k in range(len(direct_offsets))])
    others = len(plane_offsets) - 1
    wait_for(row_r2.at[pl.ds(1, others)], row_recv.at[LEVELS + 1])
    total = total + tree_sum([row_r2[k] for k in range(1, others + 1)])
    total = total / columns_total
    shift = ((at["y"] * dims["c"] + at["c"]) * dims["x"] + at["x"]) * 4
    total = pltpu.roll(jnp.broadcast_to(total, (8, 128)), 128 - shift, 1)
    total = jnp.where(iota((8, 128), 0) == iota((8, 128), 1), total, 0.0)
    out_scores[:, 0:1] = jnp.sum(total, axis=1, keepdims=True)[0:4]

    @pl.when(jnp.logical_not(head_plane))
    def _():
        wait_for(root_c, root_recv.at[1])
        out_root[...] = root_c[...]

    @pl.when(head_plane)
    def _():
        out_root[...] = root_m[...]

    planes, columns = len(plane_offsets) - 1, len(column_offsets) - 1
    for step in range(NEWTON):
        wait_for(ar_a.at[step, pl.ds(1, planes)], ar_send.at[step, 0])
        wait_for(ar_d.at[step], ar_send.at[step, 1])
        wait_for(ar_b.at[step, pl.ds(1, columns)], ar_send.at[step, 2])
    wait_for(pair_r, rs_send.at[0])
    wait_group(rs_r1, rs_send.at[1])
    wait_group(rs_r2, rs_send.at[2])
    wait_for(row_r1.at[pl.ds(1, columns)], row_send.at[0])
    wait_for(row_d, row_send.at[1])
    wait_for(row_r2.at[pl.ds(1, planes)], row_send.at[2])

    @pl.when(head_column)
    def _():
        wait_for(row_r1.at[pl.ds(1, columns)], root_send.at[0])

    @pl.when(head_plane)
    def _():
        wait_for(row_r2.at[pl.ds(1, planes)], root_send.at[1])


def on_device(
    dims,
    taxa_states,
    outside,
    children,
    branch,
    root_length,
    cat_rates,
    exchange_rates,
    frequencies,
    rivals,
    pattern_idx,
    weights,
):
    reps, columns = weights.shape
    patterns = taxa_states.shape[1]
    z, y, c, x = (dims[a] for a in ("z", "y", "c", "x"))
    tiles = x // 2
    plane, column = group_size(dims, PLANE), group_size(dims, COLUMN)
    direct = len(routes(dims)[2])
    vmem = pl.BlockSpec(memory_space=pltpu.VMEM)
    hbm = pl.BlockSpec(memory_space=pl.ANY)
    scores, loglik, root = pl.pallas_call(
        functools.partial(kernel, dims),
        out_shape=(
            jax.ShapeDtypeStruct((4, CAND), f32),
            jax.ShapeDtypeStruct((1, patterns), f32),
            jax.ShapeDtypeStruct((1, 128), f32),
        ),
        in_specs=[hbm] * 11,
        out_specs=(vmem, vmem, vmem),
        scratch_shapes=[
            pltpu.VMEM(taxa_states.shape, jnp.int32),
            pltpu.VMEM((STATES, CATS, patterns), f32),
            pltpu.SMEM((2, INNER), jnp.int32),
            pltpu.SMEM(branch.shape, f32),
            pltpu.SMEM((1, 1), f32),
            pltpu.SMEM(cat_rates.shape, f32),
            pltpu.VMEM(exchange_rates.shape, f32),
            pltpu.SMEM(frequencies.shape, f32),
            pltpu.VMEM((1, columns), jnp.int32),
            pltpu.VMEM((reps, columns), jnp.int32),
            pltpu.VMEM((RIVALS, 128), f32),
            pltpu.VMEM((reps, columns), bf16),
            pltpu.VMEM((128, columns), bf16),
            pltpu.VMEM((128, 128), f32),
            pltpu.VMEM((TERMS * PAD, 128), f32),
            pltpu.VMEM((256, 128), f32),
            pltpu.VMEM((128 * STATES, 128), f32),
            pltpu.VMEM((128 * STATES, 128), f32),
            pltpu.VMEM((128 * STATES, 128), f32),
            pltpu.VMEM((EDGES, BLOCK, 128), f32),
            pltpu.VMEM((32, 128), f32),
            pltpu.VMEM((BLOCK, 128), f32),
            pltpu.VMEM((128, CATS * 128), f32),
            pltpu.VMEM((STATES * TERMS, 128), f32),
            pltpu.VMEM((STATES, CATS, 128), f32),
            pltpu.VMEM((CATS, TERMS + 8, 128), f32),
            pltpu.VMEM((z * y, c, tiles, 8, 128), f32),
            pltpu.VMEM((z * y, tiles, 8, 128), f32),
            pltpu.VMEM((y, x, z // 2, 8, 128), f32),
            pltpu.VMEM((plane, z // 2, 8, 128), f32),
            pltpu.VMEM((z // 2, 8, 128), f32),
            pltpu.VMEM((z, 8, 128), f32),
            pltpu.VMEM((NEWTON, 1, 128), f32),
            pltpu.VMEM((NEWTON, LEVELS, 1, 128), f32),
            pltpu.VMEM((NEWTON, plane, 1, 128), f32),
            pltpu.VMEM((NEWTON, column, 1, 128), f32),
            pltpu.VMEM((NEWTON, direct, 1, 128), f32),
            pltpu.VMEM((z, 1, 128), f32),
            pltpu.VMEM((column, 1, 128), f32),
            pltpu.VMEM((LEVELS, 1, 128), f32),
            pltpu.VMEM((plane, 1, 128), f32),
            pltpu.VMEM((direct, 1, 128), f32),
            pltpu.VMEM((1, 128), f32),
            pltpu.VMEM((1, 128), f32),
            pltpu.VMEM((1, 128), f32),
            pltpu.VMEM((1, 128), f32),
            pltpu.SemaphoreType.DMA((11,)),
            pltpu.SemaphoreType.DMA((NEWTON, 3)),
            pltpu.SemaphoreType.DMA((NEWTON, LEVELS + 2)),
            pltpu.SemaphoreType.DMA((3,)),
            pltpu.SemaphoreType.DMA((3,)),
            pltpu.SemaphoreType.DMA((3,)),
            pltpu.SemaphoreType.DMA((LEVELS + 2,)),
            pltpu.SemaphoreType.DMA((2,)),
            pltpu.SemaphoreType.DMA((2,)),
        ],
        compiler_params=pltpu.CompilerParams(
            collective_id=0, has_side_effects=True, vmem_limit_bytes=63 * 1024 * 1024
        ),
    )(
        taxa_states,
        outside.transpose(1, 0, 2),
        children.T,
        branch,
        root_length.reshape(1, 1),
        cat_rates,
        exchange_rates,
        frequencies,
        pattern_idx.reshape(1, columns),
        rivals,
        weights,
    )
    return scores.T, loglik.reshape(patterns), root[0, 0:1]


def solution(mesh):
    placed = (
        P(None, ("cols", "rep")),
        P(None, None, ("cols", "rep")),
        P(),
        P(),
        P(),
        P(),
        P(),
        P(),
        P(None, ("cols", "rep")),
        P(("cols", "rep")),
        P(None, ("cols", "rep")),
    )
    return jax.shard_map(
        functools.partial(on_device, layout_of(mesh)),
        mesh=mesh,
        in_specs=placed,
        out_specs=(P(None, ("cols", "rep")), P(("cols", "rep")), P()),
        check_vma=False,
    )
```

```python
import functools
import math

import jax
import jax.numpy as jnp
from jax import lax
from jax.experimental import pallas as pl
from jax.experimental.pallas import tpu as pltpu
from jax.sharding import PartitionSpec as P

STATES = 20
CATS = 4
TERMS = 40
LEAVES = 32
INNER = 31
EDGES = 62
NEWTON = 3
RIVALS = 99
CAND = 100
MU_RATE = 4.0
LENGTH_CAP = 2.0
CORES = 2
BLOCK = CATS * STATES
PAD = 24
f32 = jnp.float32
bf16 = jnp.bfloat16
LOG_FACTORIALS = [math.lgamma(k + 1.0) for k in range(TERMS)]
MESH = pl.DeviceIdType.MESH
LEAF_UNROLL = 32
DIRECT_SLACK = 2
LEVELS = DIRECT_SLACK + 1
INNER_UNROLL = 1


def layout_of(mesh):
    cols, chips_x = mesh.shape["cols"], mesh.shape["rep"]
    chips_y = 4 if cols >= 128 else 2
    return dict(z=cols // (CORES * chips_y), y=chips_y, c=CORES, x=chips_x)


def position(dims):
    cols = lax.axis_index("cols")
    return dict(
        z=cols // (dims["y"] * dims["c"]),
        y=(cols // dims["c"]) % dims["y"],
        c=cols % dims["c"],
        x=lax.axis_index("rep"),
    )


def device_of(dims, at):
    return ((at["z"] * dims["y"] + at["y"]) * dims["c"] + at["c"], at["x"])


def group_size(dims, axes):
    return math.prod(dims[a] for a in axes)


def group_index(dims, axes, at):
    index = 0
    for a in axes:
        index = index * dims[a] + at[a]
    return index


def group_member(dims, axes, at, index):
    member = dict(at)
    for a in reversed(axes):
        member[a] = index % dims[a]
        index = index // dims[a]
    return member


def tree_sum(values):
    while len(values) > 1:
        paired = [values[i] + values[i + 1] for i in range(0, len(values) - 1, 2)]
        if len(values) % 2:
            paired.append(values[-1])
        values = paired
    return values[0]


def split_high(value):
    return value.astype(bf16).astype(f32)


def iota(shape, axis):
    return lax.broadcasted_iota(jnp.int32, shape, axis)


def pick(index, entries, base):
    chosen = base
    for number, entry in enumerate(entries):
        chosen = jnp.where(index == number, entry, chosen)
    return chosen


def ring(step, size):
    return min(step, size - step)


def routes(dims, slack):
    plane = sorted(
        ((ring(dy, dims["y"]) + ring(dx, dims["x"]), dy, dx) for dy in range(dims["y"]) for dx in range(dims["x"]))
    )
    column = sorted(((ring(dz, dims["z"]), dz, flip) for dz in range(dims["z"]) for flip in range(dims["c"])))
    most = plane[-1][0] + column[-1][0] - slack
    direct = [
        (dz, flip, dy, dx)
        for far, dz, flip in reversed(column)
        for wide, dy, dx in reversed(plane)
        if far > 0 and wide > 0 and far + wide > most
    ]

    def reach(here, limits):
        return max(other for other in limits if here == 0 or other == 0 or here + other <= most)

    wides, fars = sorted({p[0] for p in plane}), sorted({p[0] for p in column})
    column_needs = {far: reach(far, wides) for far in fars}
    plane_needs = {wide: reach(wide, fars) for wide in wides}
    return plane, column, direct, column_needs, plane_needs


PLANE = ("y", "x")
COLUMN = ("z", "c")
LINE = ("z",)


def kernel(
    dims,
    taxa_hbm,
    outside_hbm,
    children_hbm,
    branch_hbm,
    root_length_hbm,
    rates_hbm,
    exchange_hbm,
    freqs_hbm,
    pattern_hbm,
    rivals_hbm,
    weights_hbm,
    out_scores,
    out_loglik,
    out_root,
    taxa,
    outside,
    children,
    branch,
    root_length,
    rates,
    exchange,
    freqs,
    pattern,
    w_int,
    riv,
    w_b,
    onehot_b,
    square,
    powers,
    x_col,
    t_leaf,
    t_high,
    t_low,
    msg,
    largest_rows,
    prod_s,
    root_s,
    lhs_s,
    wo_s,
    m_s,
    score_s,
    pair_r,
    rs_a,
    rs_r1,
    rs_b,
    rs_r2,
    val_a,
    val_b,
    ar_a,
    ar_b,
    ar_d,
    row_v,
    row_r1,
    row_u,
    row_r2,
    row_d,
    root_a,
    root_b,
    root_c,
    root_m,
    load_sem,
    ar_send,
    ar_recv,
    rs_send,
    rs_recv,
    row_send,
    row_recv,
    root_send,
    root_recv,
):
    at = position(dims)
    reps = score_s.shape[0] * CORES * score_s.shape[2] * 8
    lanes_z = reps // dims["z"]

    loads = {}
    for number, (name, source, target) in enumerate(
        (
            ("exchange", exchange_hbm, exchange),
            ("freqs", freqs_hbm, freqs),
            ("rates", rates_hbm, rates),
            ("branch", branch_hbm, branch),
            ("taxa", taxa_hbm, taxa),
            ("children", children_hbm, children),
            ("root", root_length_hbm, root_length),
            ("outside", outside_hbm, outside),
            ("pattern", pattern_hbm, pattern),
            ("weights", weights_hbm, w_int),
            ("rivals", rivals_hbm, riv),
        )
    ):
        loads[name] = pltpu.make_async_copy(source, target, load_sem.at[number])
        loads[name].start()

    plane_offsets, column_offsets, direct_offsets, column_needs, plane_needs = routes(dims, DIRECT_SLACK)
    no_direct = routes(dims, 0)

    def peer_at(dz=0, flip=0, dy=0, dx=0):
        core = at["c"] if flip == 0 else 1 - at["c"]
        there = dict(z=(at["z"] + dz) % dims["z"], c=core, y=(at["y"] + dy) % dims["y"], x=(at["x"] + dx) % dims["x"])
        return there, device_of(dims, there)

    barrier = pltpu.get_barrier_semaphore()
    greeted = [peer_at(dz, flip)[1] for _, dz, flip in reversed(column_offsets[1:])]
    greeted += [peer_at(dy=dy, dx=dx)[1] for _, dy, dx in reversed(plane_offsets[1:])]
    for device in greeted:
        pl.semaphore_signal(barrier, inc=1, device_id=device, device_id_type=MESH)

    square[...] = jnp.zeros_like(square)
    loads["exchange"].wait()
    loads["freqs"].wait()
    square[0:STATES, 0:STATES] = exchange[...]
    full = square[...]
    symmetric = (0.5 * (full + full.T))[0:PAD]
    row24, lane24 = iota((PAD, 128), 0), iota((PAD, 128), 1)
    freq_row = pick(iota((1, 128), 1), [freqs[j] for j in range(STATES)], jnp.zeros((1, 128), f32))
    off = jnp.where(row24 == lane24, 0.0, symmetric * freq_row)
    away = jnp.sum(off, axis=1, keepdims=True)
    inside = (row24 == lane24) & (row24 < STATES)
    eye = jnp.where(inside, 1.0, jnp.zeros((PAD, 128), f32))
    stepping = eye + (off - jnp.where(inside, away, 0.0)) / MU_RATE

    def spread(block):
        twice = block + pltpu.roll(block, 20, 1)
        four = twice + pltpu.roll(twice, 40, 1)
        return jnp.where(lane24 < 80, four, pltpu.roll(four, 80, 1))

    def three_parts(value):
        high = split_high(value)
        middle = split_high(value - high)
        return high, middle, value - high - middle

    powers[0:PAD, :] = spread(eye)
    powers[PAD : 2 * PAD, :] = spread(stepping)
    lane1 = iota((1, 128), 1)
    reach = 1
    while reach < TERMS:
        count = min(reach + 1, TERMS - reach)
        high, middle, low = three_parts(powers[reach * PAD : (reach + 1) * PAD, :])
        for slot, piece in enumerate((high, middle, low, high, middle, high)):
            square[slot * STATES : (slot + 1) * STATES, :] = piece[0:STATES]
        square[120:128, :] = jnp.zeros((8, 128), f32)
        high, middle, low = three_parts(powers[0 : count * PAD, :])
        left = jnp.where(lane1 < 60, high, jnp.where(lane1 < 100, middle, jnp.where(lane1 < 120, low, 0.0)))
        powers[reach * PAD : (reach + count) * PAD, :] = jnp.dot(
            left.astype(bf16), square[...].astype(bf16), preferred_element_type=f32
        )
        reach *= 2

    loads["rates"].wait()
    loads["branch"].wait()
    row8 = iota((8, 128), 0)
    speed = [MU_RATE * rates[c] for c in range(CATS)]
    speed8 = pick(row8 % CATS, speed, jnp.zeros((8, 128), f32))
    for pair in range(EDGES // 2):
        x_col[pair * 8 : pair * 8 + 8, :] = speed8 * jnp.where(row8 < CATS, branch[2 * pair], branch[2 * pair + 1])
    x_col[EDGES * CATS :, :] = jnp.ones((8, 128), f32)
    scaled = x_col[...]
    part = (lane1 >= 40).astype(jnp.int32) + (lane1 >= 80).astype(jnp.int32) + (lane1 >= 120).astype(jnp.int32)
    order = lane1 - 40 * part
    lg_lane = pick(order, LOG_FACTORIALS, jnp.zeros((1, 128), f32))
    order = order.astype(f32)
    mixing = jnp.exp(-scaled + order * jnp.log(scaled) - lg_lane)
    mixing_high = split_high(mixing)
    mixing = jnp.where(part == 2, mixing - mixing_high, jnp.where(part == 3, 0.0, mixing_high))
    mixing = mixing.astype(bf16)

    cat128 = (lane1 >= 20).astype(jnp.int32) + (lane1 >= 40).astype(jnp.int32) + (lane1 >= 60).astype(jnp.int32)
    cat128 = jnp.where(lane1 < BLOCK, cat128, -1)
    keep = (iota((128, 1), 0) % CATS) == cat128
    lhs_part = (lane1 >= 40).astype(jnp.int32)
    lhs_part = lhs_part + (lane1 >= 80).astype(jnp.int32)
    lhs_used = (lane1 < 20) | ((lane1 >= 40) & (lane1 < 60)) | ((lane1 >= 80) & (lane1 < 100))
    for i in range(STATES):
        base = powers[pl.ds(i, TERMS, stride=PAD), :]
        base_high = split_high(base)
        base_low = base - base_high
        right = jnp.concatenate([base_high, base_low, base_high, jnp.zeros((8, 128), f32)], axis=0)
        made = jnp.dot(mixing, right.astype(bf16), preferred_element_type=f32)
        made_high = split_high(made)
        made_low = made - made_high
        t_leaf[pl.ds(i, 128, stride=STATES), :] = jnp.where(
            lane1 < 20, made_high[0:128], jnp.where(lane1 < 40, made_low[0:128], 0.0)
        )
        t_high[pl.ds(i, 128, stride=STATES), :] = jnp.where(keep, made_high[128:256], 0.0)
        t_low[pl.ds(i, 128, stride=STATES), :] = jnp.where(keep, made_low[128:256], 0.0)
        lhs_s[i * TERMS : (i + 1) * TERMS, :] = jnp.where(
            lhs_used, jnp.where(lhs_part == 1, base_low, base_high), 0.0
        )

    state48 = iota((48, 128), 0)
    state48 = jnp.where(state48 < 20, state48, jnp.where(state48 < 40, state48 - 20, -1))
    loads["taxa"].wait()

    def leaf_step(n, carry):
        hot = jnp.where(state48 == taxa[pl.ds(n, 1), :], 1.0, jnp.zeros((48, 128), f32)).astype(bf16)
        start = pl.multiple_of(n * BLOCK, 16)
        left = t_leaf[pl.ds(start, BLOCK), 0:48]
        msg[n] = jnp.dot(left.astype(bf16), hot, preferred_element_type=f32)
        return carry

    lax.fori_loop(0, LEAVES, leaf_step, 0, unroll=LEAF_UNROLL)

    largest_rows[...] = jnp.ones_like(largest_rows)
    loads["children"].wait()

    def merged(r):
        return msg[children[0, r]] * msg[children[1, r]]

    def inner_step(r, carry):
        product = merged(r)
        largest = jnp.max(product, axis=0, keepdims=True)
        largest_rows[pl.ds(r, 1), :] = largest
        high = product.astype(bf16)
        low = (product - high.astype(f32)).astype(bf16)
        start = pl.multiple_of(r * BLOCK, 16)
        left_high = t_high[pl.ds(start, BLOCK), 0:BLOCK].astype(bf16)
        left_low = t_low[pl.ds(start, BLOCK), 0:BLOCK].astype(bf16)
        both = jnp.dot(jnp.concatenate([left_high, left_low], axis=0), high, preferred_element_type=f32)
        rest = jnp.dot(left_high, low, preferred_element_type=f32)
        moved = both[0:BLOCK] + both[BLOCK:] + rest
        msg[LEAVES + r] = moved * (1.0 / largest)
        return carry

    lax.fori_loop(0, INNER - 1, inner_step, 0, unroll=INNER_UNROLL)
    product = merged(INNER - 1)
    largest = jnp.max(product, axis=0, keepdims=True)
    largest_rows[INNER - 1 : INNER, :] = largest
    prod_s[...] = product * (1.0 / largest)
    root_scale = jnp.sum(jnp.log(largest_rows[...]), axis=0, keepdims=True)

    root_s[...] = jnp.zeros_like(root_s)
    for c in range(CATS):
        piece = prod_s[c * STATES : (c + 1) * STATES, :]
        piece_high = split_high(piece)
        root_s[0:STATES, c * 128 : (c + 1) * 128] = piece_high
        root_s[40 : 40 + STATES, c * 128 : (c + 1) * 128] = piece_high
        root_s[80 : 80 + STATES, c * 128 : (c + 1) * 128] = piece - piece_high
    loads["outside"].wait()
    for i in range(STATES):
        wo_s[i] = freqs[i] * outside[i]
    root_parts = root_s[...].astype(bf16)
    lhs_b = lhs_s[...].astype(bf16)
    lifted = jnp.dot(lhs_b, root_parts, preferred_element_type=f32)
    m_s[...] = jnp.zeros_like(m_s)
    for c in range(CATS):
        basis = jnp.zeros((TERMS, 128), f32)
        for i in range(STATES):
            basis = basis + lifted[i * TERMS : (i + 1) * TERMS, c * 128 : (c + 1) * 128] * wo_s[i, c : c + 1, :]
        m_s[c, 0:TERMS, :] = basis
    order_row = iota((TERMS, 128), 0).astype(f32)
    lg_rows = jnp.concatenate(
        [pick(row8, LOG_FACTORIALS[k : k + 8], jnp.zeros((8, 128), f32)) for k in range(0, TERMS, 8)], axis=0
    )
    basis0, basis1, basis2 = [], [], []
    for c in range(CATS):
        here, next1, next2 = m_s[c, 0:TERMS, :], m_s[c, 1 : TERMS + 1, :], m_s[c, 2 : TERMS + 2, :]
        basis0.append(here)
        basis1.append(speed[c] * (next1 - here))
        basis2.append((speed[c] * speed[c]) * (next2 - 2.0 * next1 + here))

    loads["pattern"].wait()
    loads["root"].wait()
    hot = jnp.where(iota((128, 256), 0) == pattern[...], 1.0, jnp.zeros((128, 256), f32)).astype(bf16)
    onehot_b[...] = hot
    counts = lax.dot_general(
        jnp.ones((16, 256), bf16), hot, (((1,), (1,)), ((), ())), preferred_element_type=f32
    )[0:1]

    def series(length, bases):
        totals = [jnp.zeros((TERMS, 128), f32) for _ in bases]
        for c in range(CATS):
            x = speed[c] * length
            w = jnp.exp(-x + order_row * jnp.log(x) - lg_rows)
            totals = [total + w * basis[c] for total, basis in zip(totals, bases)]
        return [0.25 * jnp.sum(total, axis=0, keepdims=True) for total in totals]

    def local_sums(length):
        value, slope, bend = series(length, (basis0, basis1, basis2))
        ratio = slope / value
        return counts * ratio, counts * (bend / value - ratio * ratio)

    def send_group(axes, source, target, send, recv):
        size, mine = group_size(dims, axes), group_index(dims, axes, at)
        for step in range(1, size):
            slot = (mine + step) % size
            peer = group_member(dims, axes, at, slot)
            pltpu.make_async_remote_copy(
                src_ref=source(slot),
                dst_ref=target.at[mine],
                send_sem=send,
                recv_sem=recv,
                device_id=device_of(dims, peer),
                device_id_type=MESH,
            ).start()

    def wait_group(target, sem):
        several = target.at[pl.ds(0, target.shape[0] - 1)]
        pltpu.make_async_copy(several, several, sem).wait()

    def send(source, target, send_sem, recv_sem, device):
        pltpu.make_async_remote_copy(
            src_ref=source,
            dst_ref=target,
            send_sem=send_sem,
            recv_sem=recv_sem,
            device_id=device,
            device_id_type=MESH,
        ).start()

    def wait_for(target, sem):
        pltpu.make_async_copy(target, target, sem).wait()

    def relay(offsets, heard, heard_sems, own, needs, forward):
        total, begin = own, 1
        for level, reach in enumerate(sorted(set(needs.values()))):
            end = sum(1 for offset in offsets if offset[0] <= reach)
            if end > begin:
                wait_for(heard.at[pl.ds(begin, end - begin)], heard_sems.at[level])
                total = total + tree_sum([heard[k] for k in range(begin, end)])
                begin = end
            forward(level, [distance for distance, needed in needs.items() if needed == reach], total)
        return total

    def level_of(distance, needs):
        return min(level for level, reach in enumerate(sorted(set(needs.values()))) if distance <= reach)

    def all_sum(step, row, meanwhile, meanwhile_later):
        direct, needs = (no_direct[2], no_direct[3]) if step == 0 else (direct_offsets, column_needs)
        sems_s, sems_r = ar_send.at[step], ar_recv.at[step]
        val_a[step] = row
        for slot, (wide, dy, dx) in reversed(list(enumerate(plane_offsets))[1:]):
            level = level_of(wide, needs)
            send(val_a.at[step], ar_a.at[step, slot], sems_s.at[0], sems_r.at[level], peer_at(dy=dy, dx=dx)[1])
        for slot, offset in enumerate(direct):
            send(val_a.at[step], ar_d.at[step, slot], sems_s.at[1], sems_r.at[LEVELS], peer_at(*offset)[1])
        meanwhile()

        def forward(level, distances, total):
            val_b[step, level] = total
            for slot, (far, dz, flip) in reversed(list(enumerate(column_offsets))[1:]):
                if far in distances:
                    send(
                        val_b.at[step, level],
                        ar_b.at[step, slot],
                        sems_s.at[2],
                        sems_r.at[LEVELS + 1],
                        peer_at(dz, flip)[1],
                    )

        total = relay(plane_offsets, ar_a.at[step], sems_r, row, needs, forward)
        meanwhile_later()
        if direct:
            wait_for(ar_d.at[step], sems_r.at[LEVELS])
            total = total + tree_sum([ar_d[step, k] for k in range(len(direct))])
        others = len(column_offsets) - 1
        wait_for(ar_b.at[step, pl.ds(1, others)], sems_r.at[LEVELS + 1])
        return total + tree_sum([ar_b[step, k] for k in range(1, others + 1)])

    plane_mine = group_index(dims, PLANE, at)
    line_mine = at["z"]

    def rivals_scores():
        loads["weights"].wait()
        loads["rivals"].wait()
        w_b[...] = w_int[...].astype(f32).astype(bf16)
        rows = jnp.concatenate([riv[...], jnp.zeros((128 - RIVALS, 128), f32)], axis=0)
        high = rows.astype(bf16)
        low = (rows - high.astype(f32)).astype(bf16)
        both = jnp.concatenate([high, low], axis=0)
        gathered = jnp.dot(both, onehot_b[...], preferred_element_type=f32).astype(bf16)
        chunk = min(256, reps)
        for begin in range(0, reps, chunk):
            scores = lax.dot_general(
                w_b[begin : begin + chunk, :], gathered, (((1,), (1,)), ((), ())), preferred_element_type=f32
            )
            scores = scores[:, 0:128] + scores[:, 128:256]
            per = CORES * score_s.shape[2] * 8
            score_s[begin // per : (begin + chunk) // per] = scores.reshape(
                (chunk // per,) + score_s.shape[1:]
            )
        pltpu.make_async_remote_copy(
            src_ref=score_s.at[:, 1 - at["c"]],
            dst_ref=pair_r,
            send_sem=rs_send.at[0],
            recv_sem=rs_recv.at[0],
            device_id=device_of(dims, dict(at, c=1 - at["c"])),
            device_id_type=MESH,
        ).start()

    def rivals_plane():
        pltpu.make_async_copy(pair_r, pair_r, rs_recv.at[0]).wait()
        first_half = iota((1, 1, 8, 128), 2) < 4
        tiles = score_s.shape[2]
        chips_y = dims["y"]

        def pair_step(zp, carry):
            even_at = pl.ds(2 * zp * chips_y, chips_y)
            odd_at = pl.ds((2 * zp + 1) * chips_y, chips_y)
            even = score_s[even_at, at["c"]] + pair_r[even_at]
            odd = score_s[odd_at, at["c"]] + pair_r[odd_at]
            even_turned, odd_turned = pltpu.roll(even, 4, 2), pltpu.roll(odd, 4, 2)
            lower = jnp.where(first_half, even, odd_turned)
            upper = jnp.where(first_half, even_turned, odd)
            for t in range(tiles):
                rs_a[:, 2 * t, zp] = lower[:, t]
                rs_a[:, 2 * t + 1, zp] = upper[:, t]
            return carry

        lax.fori_loop(0, dims["z"] // 2, pair_step, 0)
        rs_r1[plane_mine] = rs_a[at["y"], at["x"]]
        send_group(
            PLANE,
            lambda slot: rs_a.at[slot // dims["x"], slot % dims["x"]],
            rs_r1,
            rs_send.at[1],
            rs_recv.at[1],
        )

    def rivals_line():
        wait_group(rs_r1, rs_recv.at[1])
        rs_b[...] = tree_sum([rs_r1[k] for k in range(rs_r1.shape[0])])
        rs_r2[line_mine] = rs_b[at["z"] // 2]
        send_group(LINE, lambda slot: rs_b.at[slot // 2], rs_r2, rs_send.at[2], rs_recv.at[2])

    columns_total = float(pattern.shape[1] * dims["z"] * dims["y"] * dims["c"] * dims["x"])

    def rivals_finish():
        wait_group(rs_r2, rs_recv.at[2])
        total = tree_sum([rs_r2[k] for k in range(rs_r2.shape[0])]) / columns_total
        total = jnp.where(at["z"] % 2 == 0, total, pltpu.roll(total, 4, 0))
        out_scores[...] = pltpu.roll(total, 1, 1)[0:4, 0:CAND]

    pl.semaphore_wait(barrier, len(greeted))
    length = jnp.full((1, 128), root_length[0, 0], f32)

    def nothing():
        return None

    hidden = [(rivals_scores, rivals_plane), (rivals_line, rivals_finish), (nothing, nothing)]
    left_half = lane1 < 64
    for step in range(NEWTON):
        first, second = local_sums(length)
        folded = jnp.where(left_half, first + pltpu.roll(first, 64, 1), second + pltpu.roll(second, 64, 1))
        sums = all_sum(step, folded, *hidden[step])
        first = jnp.sum(jnp.where(left_half, sums, 0.0), axis=1, keepdims=True)
        second = jnp.sum(jnp.where(left_half, 0.0, sums), axis=1, keepdims=True)
        proposal = length - first / jnp.minimum(second, -1.0)
        length = jnp.clip(proposal, 0.25 * length, LENGTH_CAP)

    root_a[...] = length
    head_column = (at["z"] == 0) & (at["c"] == 0)
    head_plane = (at["y"] == 0) & (at["x"] == 0)

    @pl.when(head_column)
    def _():
        root_m[...] = length
        for _, dz, flip in column_offsets[1:]:
            send(root_a, root_b, root_send.at[0], root_recv.at[0], peer_at(dz, flip)[1])


    (value,) = series(length, (basis0,))
    loglik = jnp.log(value) + root_scale
    out_loglik[...] = loglik
    high = split_high(loglik)
    middle = split_high(loglik - high)
    low = loglik - high - middle
    row16 = iota((16, 128), 0)
    parts = pick(row16, [high, middle, low], jnp.zeros((16, 128), f32)).astype(bf16)
    gathered = jnp.dot(parts, onehot_b[...], preferred_element_type=f32).astype(bf16)
    own = lax.dot_general(gathered, w_b[...], (((1,), (1,)), ((), ())), preferred_element_type=f32)
    own = jnp.sum(own, axis=0, keepdims=True)
    if lanes_z != 128:
        row_v[...] = jnp.zeros_like(row_v)
    for z in range(dims["z"]):
        row_v[z, :, 0:lanes_z] = own[:, z * lanes_z : (z + 1) * lanes_z]
    for slot, (far, dz, flip) in reversed(list(enumerate(column_offsets))[1:]):
        there, device = peer_at(dz, flip)
        level = level_of(far, plane_needs)
        send(row_v.at[there["z"]], row_r1.at[slot], row_send.at[0], row_recv.at[level], device)
    for slot, offset in enumerate(direct_offsets):
        there, device = peer_at(*offset)
        send(row_v.at[there["z"]], row_d.at[slot], row_send.at[1], row_recv.at[LEVELS], device)

    def forward_row(level, distances, total):
        row_u[level] = total
        for slot, (wide, dy, dx) in reversed(list(enumerate(plane_offsets))[1:]):
            if wide in distances:
                device = peer_at(dy=dy, dx=dx)[1]
                send(row_u.at[level], row_r2.at[slot], row_send.at[2], row_recv.at[LEVELS + 1], device)

    total = relay(column_offsets, row_r1, row_recv, row_v[at["z"]], plane_needs, forward_row)

    @pl.when(jnp.logical_not(head_column))
    def _():
        wait_for(root_b, root_recv.at[0])
        root_m[...] = root_b[...]

    @pl.when(head_plane)
    def _():
        for _, dy, dx in plane_offsets[1:]:
            send(root_m, root_c, root_send.at[1], root_recv.at[1], peer_at(dy=dy, dx=dx)[1])

    wait_for(row_d, row_recv.at[LEVELS])
    total = total + tree_sum([row_d[k] for k in range(len(direct_offsets))])
    others = len(plane_offsets) - 1
    wait_for(row_r2.at[pl.ds(1, others)], row_recv.at[LEVELS + 1])
    total = total + tree_sum([row_r2[k] for k in range(1, others + 1)])
    total = total / columns_total
    shift = ((at["y"] * dims["c"] + at["c"]) * dims["x"] + at["x"]) * 4
    total = pltpu.roll(jnp.broadcast_to(total, (8, 128)), 128 - shift, 1)
    total = jnp.where(iota((8, 128), 0) == iota((8, 128), 1), total, 0.0)
    out_scores[:, 0:1] = jnp.sum(total, axis=1, keepdims=True)[0:4]

    @pl.when(jnp.logical_not(head_plane))
    def _():
        wait_for(root_c, root_recv.at[1])
        out_root[...] = root_c[...]

    @pl.when(head_plane)
    def _():
        out_root[...] = root_m[...]

    planes, columns = len(plane_offsets) - 1, len(column_offsets) - 1
    for step in range(NEWTON):
        wait_for(ar_a.at[step, pl.ds(1, planes)], ar_send.at[step, 0])
        if step > 0:
            wait_for(ar_d.at[step], ar_send.at[step, 1])
        wait_for(ar_b.at[step, pl.ds(1, columns)], ar_send.at[step, 2])
    wait_for(pair_r, rs_send.at[0])
    wait_group(rs_r1, rs_send.at[1])
    wait_group(rs_r2, rs_send.at[2])
    wait_for(row_r1.at[pl.ds(1, columns)], row_send.at[0])
    wait_for(row_d, row_send.at[1])
    wait_for(row_r2.at[pl.ds(1, planes)], row_send.at[2])

    @pl.when(head_column)
    def _():
        wait_for(row_r1.at[pl.ds(1, columns)], root_send.at[0])

    @pl.when(head_plane)
    def _():
        wait_for(row_r2.at[pl.ds(1, planes)], root_send.at[1])


def in_hbm(value):
    return pltpu.with_memory_space_constraint(value, pltpu.HBM)


def hand_over(scores, loglik, root, out_scores, out_loglik, out_root, sems):
    copies = [
        pltpu.make_async_copy(source, target, sems.at[number])
        for number, (source, target) in enumerate(((scores, out_scores), (loglik, out_loglik), (root, out_root)))
    ]
    for copy in copies:
        copy.start()
    for copy in copies:
        copy.wait()


def on_device(
    dims,
    taxa_states,
    outside,
    children,
    branch,
    root_length,
    cat_rates,
    exchange_rates,
    frequencies,
    rivals,
    pattern_idx,
    weights,
):
    reps, columns = weights.shape
    patterns = taxa_states.shape[1]
    z, y, c, x = (dims[a] for a in ("z", "y", "c", "x"))
    tiles = x // 2
    plane, column = group_size(dims, PLANE), group_size(dims, COLUMN)
    direct = len(routes(dims, DIRECT_SLACK)[2])
    vmem = pl.BlockSpec(memory_space=pltpu.VMEM)
    hbm = pl.BlockSpec(memory_space=pl.ANY)
    scores, loglik, root = pl.pallas_call(
        functools.partial(kernel, dims),
        out_shape=(
            jax.ShapeDtypeStruct((4, CAND), f32),
            jax.ShapeDtypeStruct((1, patterns), f32),
            jax.ShapeDtypeStruct((1, 128), f32),
        ),
        in_specs=[hbm] * 11,
        out_specs=(vmem, vmem, vmem),
        scratch_shapes=[
            pltpu.VMEM(taxa_states.shape, jnp.int32),
            pltpu.VMEM((STATES, CATS, patterns), f32),
            pltpu.SMEM((2, INNER), jnp.int32),
            pltpu.SMEM(branch.shape, f32),
            pltpu.SMEM((1, 1), f32),
            pltpu.SMEM(cat_rates.shape, f32),
            pltpu.VMEM(exchange_rates.shape, f32),
            pltpu.SMEM(frequencies.shape, f32),
            pltpu.VMEM((1, columns), jnp.int32),
            pltpu.VMEM((reps, columns), jnp.int32),
            pltpu.VMEM((RIVALS, 128), f32),
            pltpu.VMEM((reps, columns), bf16),
            pltpu.VMEM((128, columns), bf16),
            pltpu.VMEM((128, 128), f32),
            pltpu.VMEM((TERMS * PAD, 128), f32),
            pltpu.VMEM((256, 128), f32),
            pltpu.VMEM((128 * STATES, 128), f32),
            pltpu.VMEM((128 * STATES, 128), f32),
            pltpu.VMEM((128 * STATES, 128), f32),
            pltpu.VMEM((EDGES, BLOCK, 128), f32),
            pltpu.VMEM((32, 128), f32),
            pltpu.VMEM((BLOCK, 128), f32),
            pltpu.VMEM((128, CATS * 128), f32),
            pltpu.VMEM((STATES * TERMS, 128), f32),
            pltpu.VMEM((STATES, CATS, 128), f32),
            pltpu.VMEM((CATS, TERMS + 8, 128), f32),
            pltpu.VMEM((z * y, c, tiles, 8, 128), f32),
            pltpu.VMEM((z * y, tiles, 8, 128), f32),
            pltpu.VMEM((y, x, z // 2, 8, 128), f32),
            pltpu.VMEM((plane, z // 2, 8, 128), f32),
            pltpu.VMEM((z // 2, 8, 128), f32),
            pltpu.VMEM((z, 8, 128), f32),
            pltpu.VMEM((NEWTON, 1, 128), f32),
            pltpu.VMEM((NEWTON, LEVELS, 1, 128), f32),
            pltpu.VMEM((NEWTON, plane, 1, 128), f32),
            pltpu.VMEM((NEWTON, column, 1, 128), f32),
            pltpu.VMEM((NEWTON, direct, 1, 128), f32),
            pltpu.VMEM((z, 1, 128), f32),
            pltpu.VMEM((column, 1, 128), f32),
            pltpu.VMEM((LEVELS, 1, 128), f32),
            pltpu.VMEM((plane, 1, 128), f32),
            pltpu.VMEM((direct, 1, 128), f32),
            pltpu.VMEM((1, 128), f32),
            pltpu.VMEM((1, 128), f32),
            pltpu.VMEM((1, 128), f32),
            pltpu.VMEM((1, 128), f32),
            pltpu.SemaphoreType.DMA((11,)),
            pltpu.SemaphoreType.DMA((NEWTON, 3)),
            pltpu.SemaphoreType.DMA((NEWTON, LEVELS + 2)),
            pltpu.SemaphoreType.DMA((3,)),
            pltpu.SemaphoreType.DMA((3,)),
            pltpu.SemaphoreType.DMA((3,)),
            pltpu.SemaphoreType.DMA((LEVELS + 2,)),
            pltpu.SemaphoreType.DMA((2,)),
            pltpu.SemaphoreType.DMA((2,)),
        ],
        compiler_params=pltpu.CompilerParams(
            collective_id=0, has_side_effects=True, vmem_limit_bytes=40 * 1024 * 1024
        ),
    )(
        in_hbm(taxa_states),
        in_hbm(outside.transpose(1, 0, 2)),
        in_hbm(children.T),
        in_hbm(branch),
        root_length.reshape(1, 1),
        in_hbm(cat_rates),
        in_hbm(exchange_rates),
        in_hbm(frequencies),
        in_hbm(pattern_idx.reshape(1, columns)),
        in_hbm(rivals),
        in_hbm(weights),
    )
    scores, loglik, root = pl.pallas_call(
        hand_over,
        out_shape=(
            jax.ShapeDtypeStruct((4, CAND), f32),
            jax.ShapeDtypeStruct((1, patterns), f32),
            jax.ShapeDtypeStruct((1, 128), f32),
        ),
        in_specs=[hbm] * 3,
        out_specs=(pl.BlockSpec(memory_space=pltpu.HBM),) * 3,
        scratch_shapes=[pltpu.SemaphoreType.DMA((3,))],
        compiler_params=pltpu.CompilerParams(vmem_limit_bytes=16 * 1024 * 1024),
    )(scores, loglik, root)
    return scores.T, loglik.reshape(patterns), root[0, 0:1]


def solution(mesh):
    placed = (
        P(None, ("cols", "rep")),
        P(None, None, ("cols", "rep")),
        P(),
        P(),
        P(),
        P(),
        P(),
        P(),
        P(None, ("cols", "rep")),
        P(("cols", "rep")),
        P(None, ("cols", "rep")),
    )
    return jax.shard_map(
        functools.partial(on_device, layout_of(mesh)),
        mesh=mesh,
        in_specs=placed,
        out_specs=(P(None, ("cols", "rep")), P(("cols", "rep")), P()),
        check_vma=False,
    )
```

```python
import functools
import math

import jax
import jax.numpy as jnp
from jax import lax
from jax.experimental import pallas as pl
from jax.experimental.pallas import tpu as pltpu
from jax.sharding import PartitionSpec as P

STATES = 20
CATS = 4
TERMS = 40
LEAVES = 32
INNER = 31
EDGES = 62
NEWTON = 3
RIVALS = 99
CAND = 100
MU_RATE = 4.0
LENGTH_CAP = 2.0
CORES = 2
BLOCK = CATS * STATES
PAD = 24
f32 = jnp.float32
bf16 = jnp.bfloat16
LOG_FACTORIALS = [math.lgamma(k + 1.0) for k in range(TERMS)]
MESH = pl.DeviceIdType.MESH
LEAF_UNROLL = 32
DIRECT_SLACK = 2
LEVELS = DIRECT_SLACK + 1
INNER_UNROLL = 1


def layout_of(mesh):
    cols, chips_x = mesh.shape["cols"], mesh.shape["rep"]
    chips_y = 4 if cols >= 128 else 2
    return dict(z=cols // (CORES * chips_y), y=chips_y, c=CORES, x=chips_x)


def position(dims):
    cols = lax.axis_index("cols")
    return dict(
        z=cols // (dims["y"] * dims["c"]),
        y=(cols // dims["c"]) % dims["y"],
        c=cols % dims["c"],
        x=lax.axis_index("rep"),
    )


def device_of(dims, at):
    return ((at["z"] * dims["y"] + at["y"]) * dims["c"] + at["c"], at["x"])


def group_size(dims, axes):
    return math.prod(dims[a] for a in axes)


def group_index(dims, axes, at):
    index = 0
    for a in axes:
        index = index * dims[a] + at[a]
    return index


def group_member(dims, axes, at, index):
    member = dict(at)
    for a in reversed(axes):
        member[a] = index % dims[a]
        index = index // dims[a]
    return member


def tree_sum(values):
    while len(values) > 1:
        paired = [values[i] + values[i + 1] for i in range(0, len(values) - 1, 2)]
        if len(values) % 2:
            paired.append(values[-1])
        values = paired
    return values[0]


def split_high(value):
    return value.astype(bf16).astype(f32)


def iota(shape, axis):
    return lax.broadcasted_iota(jnp.int32, shape, axis)


def pick(index, entries, base):
    chosen = base
    for number, entry in enumerate(entries):
        chosen = jnp.where(index == number, entry, chosen)
    return chosen


def ring(step, size):
    return min(step, size - step)


def routes(dims, slack):
    plane = sorted(
        ((ring(dy, dims["y"]) + ring(dx, dims["x"]), dy, dx) for dy in range(dims["y"]) for dx in range(dims["x"]))
    )
    column = sorted(((ring(dz, dims["z"]), dz, flip) for dz in range(dims["z"]) for flip in range(dims["c"])))
    most = plane[-1][0] + column[-1][0] - slack
    direct = [
        (dz, flip, dy, dx)
        for far, dz, flip in reversed(column)
        for wide, dy, dx in reversed(plane)
        if far > 0 and wide > 0 and far + wide > most
    ]

    def reach(here, limits):
        return max(other for other in limits if here == 0 or other == 0 or here + other <= most)

    wides, fars = sorted({p[0] for p in plane}), sorted({p[0] for p in column})
    column_needs = {far: reach(far, wides) for far in fars}
    plane_needs = {wide: reach(wide, fars) for wide in wides}
    return plane, column, direct, column_needs, plane_needs


PLANE = ("y", "x")
COLUMN = ("z", "c")
LINE = ("z",)


def kernel(
    dims,
    taxa_hbm,
    outside_hbm,
    children_hbm,
    branch_hbm,
    root_length_hbm,
    rates_hbm,
    exchange_hbm,
    freqs_hbm,
    pattern_hbm,
    rivals_hbm,
    weights_hbm,
    out_scores,
    out_loglik,
    out_root,
    taxa,
    outside,
    children,
    branch,
    root_length,
    rates,
    exchange,
    freqs,
    pattern,
    w_int,
    riv,
    w_b,
    onehot_b,
    tallies,
    square,
    powers,
    x_col,
    t_leaf,
    t_high,
    t_low,
    msg,
    largest_rows,
    prod_s,
    root_s,
    lhs_s,
    wo_s,
    m_s,
    score_s,
    pair_r,
    rs_a,
    rs_r1,
    rs_b,
    rs_r2,
    val_a,
    val_b,
    ar_a,
    ar_b,
    ar_d,
    row_v,
    row_r1,
    row_u,
    row_r2,
    row_d,
    root_a,
    root_b,
    root_c,
    root_m,
    load_sem,
    ar_send,
    ar_recv,
    rs_send,
    rs_recv,
    row_send,
    row_recv,
    root_send,
    root_recv,
):
    at = position(dims)
    reps = score_s.shape[0] * CORES * score_s.shape[2] * 8
    lanes_z = reps // dims["z"]

    loads = {}
    for number, (name, source, target) in enumerate(
        (
            ("exchange", exchange_hbm, exchange),
            ("freqs", freqs_hbm, freqs),
            ("rates", rates_hbm, rates),
            ("branch", branch_hbm, branch),
            ("taxa", taxa_hbm, taxa),
            ("children", children_hbm, children),
            ("root", root_length_hbm, root_length),
            ("outside", outside_hbm, outside),
            ("pattern", pattern_hbm, pattern),
            ("weights", weights_hbm, w_int),
            ("rivals", rivals_hbm, riv),
        )
    ):
        loads[name] = pltpu.make_async_copy(source, target, load_sem.at[number])
        loads[name].start()

    plane_offsets, column_offsets, direct_offsets, column_needs, plane_needs = routes(dims, DIRECT_SLACK)
    no_direct = routes(dims, 0)

    def peer_at(dz=0, flip=0, dy=0, dx=0):
        core = at["c"] if flip == 0 else 1 - at["c"]
        there = dict(z=(at["z"] + dz) % dims["z"], c=core, y=(at["y"] + dy) % dims["y"], x=(at["x"] + dx) % dims["x"])
        return there, device_of(dims, there)

    barrier = pltpu.get_barrier_semaphore()
    greeted = [peer_at(dz, flip)[1] for _, dz, flip in reversed(column_offsets[1:])]
    greeted += [peer_at(dy=dy, dx=dx)[1] for _, dy, dx in reversed(plane_offsets[1:])]
    for device in greeted:
        pl.semaphore_signal(barrier, inc=1, device_id=device, device_id_type=MESH)

    square[...] = jnp.zeros_like(square)
    loads["exchange"].wait()
    loads["freqs"].wait()
    square[0:STATES, 0:STATES] = exchange[...]
    full = square[...]
    symmetric = (0.5 * (full + full.T))[0:PAD]
    row24, lane24 = iota((PAD, 128), 0), iota((PAD, 128), 1)
    freq_row = pick(iota((1, 128), 1), [freqs[j] for j in range(STATES)], jnp.zeros((1, 128), f32))
    off = jnp.where(row24 == lane24, 0.0, symmetric * freq_row)
    away = jnp.sum(off, axis=1, keepdims=True)
    inside = (row24 == lane24) & (row24 < STATES)
    eye = jnp.where(inside, 1.0, jnp.zeros((PAD, 128), f32))
    stepping = eye + (off - jnp.where(inside, away, 0.0)) / MU_RATE

    def spread(block):
        twice = block + pltpu.roll(block, 20, 1)
        four = twice + pltpu.roll(twice, 40, 1)
        return jnp.where(lane24 < 80, four, pltpu.roll(four, 80, 1))

    def three_parts(value):
        high = split_high(value)
        middle = split_high(value - high)
        return high, middle, value - high - middle

    powers[0:PAD, :] = spread(eye)
    powers[PAD : 2 * PAD, :] = spread(stepping)
    lane1 = iota((1, 128), 1)
    reach = 1
    while reach < TERMS:
        count = min(reach + 1, TERMS - reach)
        high, middle, low = three_parts(powers[reach * PAD : (reach + 1) * PAD, :])
        for slot, piece in enumerate((high, middle, low, high, middle, high)):
            square[slot * STATES : (slot + 1) * STATES, :] = piece[0:STATES]
        square[120:128, :] = jnp.zeros((8, 128), f32)
        high, middle, low = three_parts(powers[0 : count * PAD, :])
        left = jnp.where(lane1 < 60, high, jnp.where(lane1 < 100, middle, jnp.where(lane1 < 120, low, 0.0)))
        powers[reach * PAD : (reach + count) * PAD, :] = jnp.dot(
            left.astype(bf16), square[...].astype(bf16), preferred_element_type=f32
        )
        reach *= 2

    loads["rates"].wait()
    loads["branch"].wait()
    row8 = iota((8, 128), 0)
    speed = [MU_RATE * rates[c] for c in range(CATS)]
    speed8 = pick(row8 % CATS, speed, jnp.zeros((8, 128), f32))
    for pair in range(EDGES // 2):
        x_col[pair * 8 : pair * 8 + 8, :] = speed8 * jnp.where(row8 < CATS, branch[2 * pair], branch[2 * pair + 1])
    x_col[EDGES * CATS :, :] = jnp.ones((8, 128), f32)
    scaled = x_col[...]
    part = (lane1 >= 40).astype(jnp.int32) + (lane1 >= 80).astype(jnp.int32) + (lane1 >= 120).astype(jnp.int32)
    order = lane1 - 40 * part
    lg_lane = pick(order, LOG_FACTORIALS, jnp.zeros((1, 128), f32))
    order = order.astype(f32)
    mixing = jnp.exp(-scaled + order * jnp.log(scaled) - lg_lane)
    mixing_high = split_high(mixing)
    mixing = jnp.where(part == 2, mixing - mixing_high, jnp.where(part == 3, 0.0, mixing_high))
    mixing = mixing.astype(bf16)

    cat128 = (lane1 >= 20).astype(jnp.int32) + (lane1 >= 40).astype(jnp.int32) + (lane1 >= 60).astype(jnp.int32)
    cat128 = jnp.where(lane1 < BLOCK, cat128, -1)
    keep = (iota((128, 1), 0) % CATS) == cat128
    lhs_part = (lane1 >= 40).astype(jnp.int32)
    lhs_part = lhs_part + (lane1 >= 80).astype(jnp.int32)
    lhs_used = (lane1 < 20) | ((lane1 >= 40) & (lane1 < 60)) | ((lane1 >= 80) & (lane1 < 100))
    for i in range(STATES):
        base = powers[pl.ds(i, TERMS, stride=PAD), :]
        base_high = split_high(base)
        base_low = base - base_high
        right = jnp.concatenate([base_high, base_low, base_high, jnp.zeros((8, 128), f32)], axis=0)
        made = jnp.dot(mixing, right.astype(bf16), preferred_element_type=f32)
        made_high = split_high(made)
        made_low = made - made_high
        t_leaf[pl.ds(i, 128, stride=STATES), :] = jnp.where(
            lane1 < 20, made_high[0:128], jnp.where(lane1 < 40, made_low[0:128], 0.0)
        )
        t_high[pl.ds(i, 128, stride=STATES), :] = jnp.where(keep, made_high[128:256], 0.0)
        t_low[pl.ds(i, 128, stride=STATES), :] = jnp.where(keep, made_low[128:256], 0.0)
        lhs_s[i * TERMS : (i + 1) * TERMS, :] = jnp.where(
            lhs_used, jnp.where(lhs_part == 1, base_low, base_high), 0.0
        )

    state48 = iota((48, 128), 0)
    state48 = jnp.where(state48 < 20, state48, jnp.where(state48 < 40, state48 - 20, -1))
    loads["taxa"].wait()

    def leaf_step(n, carry):
        hot = jnp.where(state48 == taxa[pl.ds(n, 1), :], 1.0, jnp.zeros((48, 128), f32)).astype(bf16)
        start = pl.multiple_of(n * BLOCK, 16)
        left = t_leaf[pl.ds(start, BLOCK), 0:48]
        msg[n] = jnp.dot(left.astype(bf16), hot, preferred_element_type=f32)
        return carry

    lax.fori_loop(0, LEAVES, leaf_step, 0, unroll=LEAF_UNROLL)

    largest_rows[...] = jnp.ones_like(largest_rows)
    loads["children"].wait()

    def merged(r):
        return msg[children[0, r]] * msg[children[1, r]]

    def inner_step(r, carry):
        product = merged(r)
        largest = jnp.max(product, axis=0, keepdims=True)
        largest_rows[pl.ds(r, 1), :] = largest
        high = product.astype(bf16)
        low = (product - high.astype(f32)).astype(bf16)
        start = pl.multiple_of(r * BLOCK, 16)
        left_high = t_high[pl.ds(start, BLOCK), 0:BLOCK].astype(bf16)
        left_low = t_low[pl.ds(start, BLOCK), 0:BLOCK].astype(bf16)
        both = jnp.dot(jnp.concatenate([left_high, left_low], axis=0), high, preferred_element_type=f32)
        rest = jnp.dot(left_high, low, preferred_element_type=f32)
        moved = both[0:BLOCK] + both[BLOCK:] + rest
        msg[LEAVES + r] = moved * (1.0 / largest)
        return carry

    lax.fori_loop(0, INNER - 1, inner_step, 0, unroll=INNER_UNROLL)
    product = merged(INNER - 1)
    largest = jnp.max(product, axis=0, keepdims=True)
    largest_rows[INNER - 1 : INNER, :] = largest
    prod_s[...] = product * (1.0 / largest)
    root_scale = jnp.sum(jnp.log(largest_rows[...]), axis=0, keepdims=True)

    root_s[...] = jnp.zeros_like(root_s)
    for c in range(CATS):
        piece = prod_s[c * STATES : (c + 1) * STATES, :]
        piece_high = split_high(piece)
        root_s[0:STATES, c * 128 : (c + 1) * 128] = piece_high
        root_s[40 : 40 + STATES, c * 128 : (c + 1) * 128] = piece_high
        root_s[80 : 80 + STATES, c * 128 : (c + 1) * 128] = piece - piece_high
    loads["outside"].wait()
    for i in range(STATES):
        wo_s[i] = freqs[i] * outside[i]
    root_parts = root_s[...].astype(bf16)
    lhs_b = lhs_s[...].astype(bf16)
    lifted = jnp.dot(lhs_b, root_parts, preferred_element_type=f32)
    m_s[...] = jnp.zeros_like(m_s)
    for c in range(CATS):
        basis = jnp.zeros((TERMS, 128), f32)
        for i in range(STATES):
            basis = basis + lifted[i * TERMS : (i + 1) * TERMS, c * 128 : (c + 1) * 128] * wo_s[i, c : c + 1, :]
        m_s[c, 0:TERMS, :] = basis
    order_row = iota((TERMS, 128), 0).astype(f32)
    lg_rows = jnp.concatenate(
        [pick(row8, LOG_FACTORIALS[k : k + 8], jnp.zeros((8, 128), f32)) for k in range(0, TERMS, 8)], axis=0
    )
    basis0, basis1, basis2 = [], [], []
    for c in range(CATS):
        here, next1, next2 = m_s[c, 0:TERMS, :], m_s[c, 1 : TERMS + 1, :], m_s[c, 2 : TERMS + 2, :]
        basis0.append(here)
        basis1.append(speed[c] * (next1 - here))
        basis2.append((speed[c] * speed[c]) * (next2 - 2.0 * next1 + here))

    loads["pattern"].wait()
    loads["root"].wait()
    hot = jnp.where(iota((128, 256), 0) == pattern[...], 1.0, jnp.zeros((128, 256), f32)).astype(bf16)
    onehot_b[...] = hot
    counts = lax.dot_general(
        jnp.ones((16, 256), bf16), hot, (((1,), (1,)), ((), ())), preferred_element_type=f32
    )[0:1]

    def series(length, bases):
        totals = [jnp.zeros((TERMS, 128), f32) for _ in bases]
        for c in range(CATS):
            x = speed[c] * length
            w = jnp.exp(-x + order_row * jnp.log(x) - lg_rows)
            totals = [total + w * basis[c] for total, basis in zip(totals, bases)]
        return [0.25 * jnp.sum(total, axis=0, keepdims=True) for total in totals]

    def local_sums(length):
        value, slope, bend = series(length, (basis0, basis1, basis2))
        ratio = slope / value
        return counts * ratio, counts * (bend / value - ratio * ratio)

    def send_group(axes, source, target, send, recv):
        size, mine = group_size(dims, axes), group_index(dims, axes, at)
        for step in range(1, size):
            slot = (mine + step) % size
            peer = group_member(dims, axes, at, slot)
            pltpu.make_async_remote_copy(
                src_ref=source(slot),
                dst_ref=target.at[mine],
                send_sem=send,
                recv_sem=recv,
                device_id=device_of(dims, peer),
                device_id_type=MESH,
            ).start()

    def wait_group(target, sem):
        several = target.at[pl.ds(0, target.shape[0] - 1)]
        pltpu.make_async_copy(several, several, sem).wait()

    def send(source, target, send_sem, recv_sem, device):
        pltpu.make_async_remote_copy(
            src_ref=source,
            dst_ref=target,
            send_sem=send_sem,
            recv_sem=recv_sem,
            device_id=device,
            device_id_type=MESH,
        ).start()

    def wait_for(target, sem):
        pltpu.make_async_copy(target, target, sem).wait()

    def relay(offsets, heard, heard_sems, own, needs, forward):
        total, begin = own, 1
        for level, reach in enumerate(sorted(set(needs.values()))):
            end = sum(1 for offset in offsets if offset[0] <= reach)
            if end > begin:
                wait_for(heard.at[pl.ds(begin, end - begin)], heard_sems.at[level])
                total = total + tree_sum([heard[k] for k in range(begin, end)])
                begin = end
            forward(level, [distance for distance, needed in needs.items() if needed == reach], total)
        return total

    def level_of(distance, needs):
        return min(level for level, reach in enumerate(sorted(set(needs.values()))) if distance <= reach)

    def all_sum(step, row, meanwhile, meanwhile_later):
        direct, needs = (no_direct[2], no_direct[3]) if step == 0 else (direct_offsets, column_needs)
        sems_s, sems_r = ar_send.at[step], ar_recv.at[step]
        val_a[step] = row
        for slot, (wide, dy, dx) in reversed(list(enumerate(plane_offsets))[1:]):
            level = level_of(wide, needs)
            send(val_a.at[step], ar_a.at[step, slot], sems_s.at[0], sems_r.at[level], peer_at(dy=dy, dx=dx)[1])
        for slot, offset in enumerate(direct):
            send(val_a.at[step], ar_d.at[step, slot], sems_s.at[1], sems_r.at[LEVELS], peer_at(*offset)[1])
        meanwhile()

        def forward(level, distances, total):
            val_b[step, level] = total
            for slot, (far, dz, flip) in reversed(list(enumerate(column_offsets))[1:]):
                if far in distances:
                    send(
                        val_b.at[step, level],
                        ar_b.at[step, slot],
                        sems_s.at[2],
                        sems_r.at[LEVELS + 1],
                        peer_at(dz, flip)[1],
                    )

        total = relay(plane_offsets, ar_a.at[step], sems_r, row, needs, forward)
        meanwhile_later()
        if direct:
            wait_for(ar_d.at[step], sems_r.at[LEVELS])
            total = total + tree_sum([ar_d[step, k] for k in range(len(direct))])
        others = len(column_offsets) - 1
        wait_for(ar_b.at[step, pl.ds(1, others)], sems_r.at[LEVELS + 1])
        return total + tree_sum([ar_b[step, k] for k in range(1, others + 1)])

    plane_mine = group_index(dims, PLANE, at)
    line_mine = at["z"]

    def rivals_scores():
        loads["weights"].wait()
        loads["rivals"].wait()
        w_b[...] = w_int[...].astype(f32).astype(bf16)
        rows = jnp.concatenate([riv[...], jnp.zeros((128 - RIVALS, 128), f32)], axis=0)
        high = rows.astype(bf16)
        low = (rows - high.astype(f32)).astype(bf16)
        both = jnp.concatenate([high, low], axis=0)
        gathered = jnp.dot(both, onehot_b[...], preferred_element_type=f32).astype(bf16)
        chunk = min(256, reps)
        for begin in range(0, reps, chunk):
            scores = lax.dot_general(
                w_b[begin : begin + chunk, :], gathered, (((1,), (1,)), ((), ())), preferred_element_type=f32
            )
            scores = scores[:, 0:128] + scores[:, 128:256]
            per = CORES * score_s.shape[2] * 8
            score_s[begin // per : (begin + chunk) // per] = scores.reshape(
                (chunk // per,) + score_s.shape[1:]
            )
        pltpu.make_async_remote_copy(
            src_ref=score_s.at[:, 1 - at["c"]],
            dst_ref=pair_r,
            send_sem=rs_send.at[0],
            recv_sem=rs_recv.at[0],
            device_id=device_of(dims, dict(at, c=1 - at["c"])),
            device_id_type=MESH,
        ).start()

    def rivals_plane():
        pltpu.make_async_copy(pair_r, pair_r, rs_recv.at[0]).wait()
        first_half = iota((1, 1, 8, 128), 2) < 4
        tiles = score_s.shape[2]
        chips_y = dims["y"]

        def pair_step(zp, carry):
            even_at = pl.ds(2 * zp * chips_y, chips_y)
            odd_at = pl.ds((2 * zp + 1) * chips_y, chips_y)
            even = score_s[even_at, at["c"]] + pair_r[even_at]
            odd = score_s[odd_at, at["c"]] + pair_r[odd_at]
            even_turned, odd_turned = pltpu.roll(even, 4, 2), pltpu.roll(odd, 4, 2)
            lower = jnp.where(first_half, even, odd_turned)
            upper = jnp.where(first_half, even_turned, odd)
            for t in range(tiles):
                rs_a[:, 2 * t, zp] = lower[:, t]
                rs_a[:, 2 * t + 1, zp] = upper[:, t]
            return carry

        lax.fori_loop(0, dims["z"] // 2, pair_step, 0)
        rs_r1[plane_mine] = rs_a[at["y"], at["x"]]
        send_group(
            PLANE,
            lambda slot: rs_a.at[slot // dims["x"], slot % dims["x"]],
            rs_r1,
            rs_send.at[1],
            rs_recv.at[1],
        )

    def rivals_line():
        wait_group(rs_r1, rs_recv.at[1])
        rs_b[...] = tree_sum([rs_r1[k] for k in range(rs_r1.shape[0])])
        rs_r2[line_mine] = rs_b[at["z"] // 2]
        send_group(LINE, lambda slot: rs_b.at[slot // 2], rs_r2, rs_send.at[2], rs_recv.at[2])

    columns_total = float(pattern.shape[1] * dims["z"] * dims["y"] * dims["c"] * dims["x"])

    def rivals_finish():
        wait_group(rs_r2, rs_recv.at[2])
        total = tree_sum([rs_r2[k] for k in range(rs_r2.shape[0])]) / columns_total
        total = jnp.where(at["z"] % 2 == 0, total, pltpu.roll(total, 4, 0))
        out_scores[...] = pltpu.roll(total, 1, 1)[0:4, 0:CAND]

    pl.semaphore_wait(barrier, len(greeted))
    length = jnp.full((1, 128), root_length[0, 0], f32)

    def pattern_tallies():
        chunk = min(256, reps)
        for begin in range(0, reps, chunk):
            made = lax.dot_general(
                onehot_b[...], w_b[begin : begin + chunk, :], (((1,), (1,)), ((), ())), preferred_element_type=f32
            )
            high = made.astype(bf16)
            tallies[0:128, begin : begin + chunk] = high
            tallies[128:256, begin : begin + chunk] = (made - high.astype(f32)).astype(bf16)

    def nothing():
        return None

    hidden = [(rivals_scores, rivals_plane), (rivals_line, rivals_finish), (pattern_tallies, nothing)]
    left_half = lane1 < 64
    for step in range(NEWTON):
        first, second = local_sums(length)
        folded = jnp.where(left_half, first + pltpu.roll(first, 64, 1), second + pltpu.roll(second, 64, 1))
        sums = all_sum(step, folded, *hidden[step])
        first = jnp.sum(jnp.where(left_half, sums, 0.0), axis=1, keepdims=True)
        second = jnp.sum(jnp.where(left_half, 0.0, sums), axis=1, keepdims=True)
        proposal = length - first / jnp.minimum(second, -1.0)
        length = jnp.clip(proposal, 0.25 * length, LENGTH_CAP)

    root_a[...] = length
    head_column = (at["z"] == 0) & (at["c"] == 0)
    head_plane = (at["y"] == 0) & (at["x"] == 0)

    @pl.when(head_column)
    def _():
        root_m[...] = length
        for _, dz, flip in reversed(column_offsets[1:]):
            send(root_a, root_b, root_send.at[0], root_recv.at[0], peer_at(dz, flip)[1])


    (value,) = series(length, (basis0,))
    loglik = jnp.log(value) + root_scale
    out_loglik[...] = loglik
    high = split_high(loglik)
    middle = split_high(loglik - high)
    low = loglik - high - middle
    row16 = iota((16, 128), 0)
    parts = pick(row16, [high, middle, low], jnp.zeros((16, 128), f32)).astype(bf16)
    own = jnp.dot(jnp.concatenate([parts, parts], axis=1), tallies[...], preferred_element_type=f32)
    own = jnp.sum(own[0:8], axis=0, keepdims=True)
    if lanes_z != 128:
        row_v[...] = jnp.zeros_like(row_v)
    for z in range(dims["z"]):
        row_v[z, :, 0:lanes_z] = own[:, z * lanes_z : (z + 1) * lanes_z]
    for slot, (far, dz, flip) in reversed(list(enumerate(column_offsets))[1:]):
        there, device = peer_at(dz, flip)
        level = level_of(far, plane_needs)
        send(row_v.at[there["z"]], row_r1.at[slot], row_send.at[0], row_recv.at[level], device)
    for slot, offset in enumerate(direct_offsets):
        there, device = peer_at(*offset)
        send(row_v.at[there["z"]], row_d.at[slot], row_send.at[1], row_recv.at[LEVELS], device)

    def pass_root_on():
        @pl.when(jnp.logical_not(head_column))
        def _():
            wait_for(root_b, root_recv.at[0])
            root_m[...] = root_b[...]

        @pl.when(head_plane)
        def _():
            for _, dy, dx in reversed(plane_offsets[1:]):
                send(root_m, root_c, root_send.at[1], root_recv.at[1], peer_at(dy=dy, dx=dx)[1])

    def forward_row(level, distances, total):
        row_u[level] = total
        for slot, (wide, dy, dx) in reversed(list(enumerate(plane_offsets))[1:]):
            if wide in distances:
                device = peer_at(dy=dy, dx=dx)[1]
                send(row_u.at[level], row_r2.at[slot], row_send.at[2], row_recv.at[LEVELS + 1], device)
        if level == 0:
            pass_root_on()

    total = relay(column_offsets, row_r1, row_recv, row_v[at["z"]], plane_needs, forward_row)

    wait_for(row_d, row_recv.at[LEVELS])
    total = total + tree_sum([row_d[k] for k in range(len(direct_offsets))])
    others = len(plane_offsets) - 1
    wait_for(row_r2.at[pl.ds(1, others)], row_recv.at[LEVELS + 1])
    total = total + tree_sum([row_r2[k] for k in range(1, others + 1)])
    total = total / columns_total
    shift = ((at["y"] * dims["c"] + at["c"]) * dims["x"] + at["x"]) * 4
    total = pltpu.roll(jnp.broadcast_to(total, (8, 128)), 128 - shift, 1)
    total = jnp.where(iota((8, 128), 0) == iota((8, 128), 1), total, 0.0)
    out_scores[:, 0:1] = jnp.sum(total, axis=1, keepdims=True)[0:4]

    @pl.when(jnp.logical_not(head_plane))
    def _():
        wait_for(root_c, root_recv.at[1])
        out_root[...] = root_c[...]

    @pl.when(head_plane)
    def _():
        out_root[...] = root_m[...]

    planes, columns = len(plane_offsets) - 1, len(column_offsets) - 1
    for step in range(NEWTON):
        wait_for(ar_a.at[step, pl.ds(1, planes)], ar_send.at[step, 0])
        if step > 0:
            wait_for(ar_d.at[step], ar_send.at[step, 1])
        wait_for(ar_b.at[step, pl.ds(1, columns)], ar_send.at[step, 2])
    wait_for(pair_r, rs_send.at[0])
    wait_group(rs_r1, rs_send.at[1])
    wait_group(rs_r2, rs_send.at[2])
    wait_for(row_r1.at[pl.ds(1, columns)], row_send.at[0])
    wait_for(row_d, row_send.at[1])
    wait_for(row_r2.at[pl.ds(1, planes)], row_send.at[2])

    @pl.when(head_column)
    def _():
        wait_for(row_r1.at[pl.ds(1, columns)], root_send.at[0])

    @pl.when(head_plane)
    def _():
        wait_for(row_r2.at[pl.ds(1, planes)], root_send.at[1])


def in_hbm(value):
    return pltpu.with_memory_space_constraint(value, pltpu.HBM)


def hand_over(scores, loglik, root, out_scores, out_loglik, out_root, sems):
    copies = [
        pltpu.make_async_copy(source, target, sems.at[number])
        for number, (source, target) in enumerate(((scores, out_scores), (loglik, out_loglik), (root, out_root)))
    ]
    for copy in copies:
        copy.start()
    for copy in copies:
        copy.wait()


def on_device(
    dims,
    taxa_states,
    outside,
    children,
    branch,
    root_length,
    cat_rates,
    exchange_rates,
    frequencies,
    rivals,
    pattern_idx,
    weights,
):
    reps, columns = weights.shape
    patterns = taxa_states.shape[1]
    z, y, c, x = (dims[a] for a in ("z", "y", "c", "x"))
    tiles = x // 2
    plane, column = group_size(dims, PLANE), group_size(dims, COLUMN)
    direct = len(routes(dims, DIRECT_SLACK)[2])
    vmem = pl.BlockSpec(memory_space=pltpu.VMEM)
    hbm = pl.BlockSpec(memory_space=pl.ANY)
    scores, loglik, root = pl.pallas_call(
        functools.partial(kernel, dims),
        out_shape=(
            jax.ShapeDtypeStruct((4, CAND), f32),
            jax.ShapeDtypeStruct((1, patterns), f32),
            jax.ShapeDtypeStruct((1, 128), f32),
        ),
        in_specs=[hbm] * 11,
        out_specs=(vmem, vmem, vmem),
        scratch_shapes=[
            pltpu.VMEM(taxa_states.shape, jnp.int32),
            pltpu.VMEM((STATES, CATS, patterns), f32),
            pltpu.SMEM((2, INNER), jnp.int32),
            pltpu.SMEM(branch.shape, f32),
            pltpu.SMEM((1, 1), f32),
            pltpu.SMEM(cat_rates.shape, f32),
            pltpu.VMEM(exchange_rates.shape, f32),
            pltpu.SMEM(frequencies.shape, f32),
            pltpu.VMEM((1, columns), jnp.int32),
            pltpu.VMEM((reps, columns), jnp.int32),
            pltpu.VMEM((RIVALS, 128), f32),
            pltpu.VMEM((reps, columns), bf16),
            pltpu.VMEM((128, columns), bf16),
            pltpu.VMEM((256, reps), bf16),
            pltpu.VMEM((128, 128), f32),
            pltpu.VMEM((TERMS * PAD, 128), f32),
            pltpu.VMEM((256, 128), f32),
            pltpu.VMEM((128 * STATES, 128), f32),
            pltpu.VMEM((128 * STATES, 128), f32),
            pltpu.VMEM((128 * STATES, 128), f32),
            pltpu.VMEM((EDGES, BLOCK, 128), f32),
            pltpu.VMEM((32, 128), f32),
            pltpu.VMEM((BLOCK, 128), f32),
            pltpu.VMEM((128, CATS * 128), f32),
            pltpu.VMEM((STATES * TERMS, 128), f32),
            pltpu.VMEM((STATES, CATS, 128), f32),
            pltpu.VMEM((CATS, TERMS + 8, 128), f32),
            pltpu.VMEM((z * y, c, tiles, 8, 128), f32),
            pltpu.VMEM((z * y, tiles, 8, 128), f32),
            pltpu.VMEM((y, x, z // 2, 8, 128), f32),
            pltpu.VMEM((plane, z // 2, 8, 128), f32),
            pltpu.VMEM((z // 2, 8, 128), f32),
            pltpu.VMEM((z, 8, 128), f32),
            pltpu.VMEM((NEWTON, 1, 128), f32),
            pltpu.VMEM((NEWTON, LEVELS, 1, 128), f32),
            pltpu.VMEM((NEWTON, plane, 1, 128), f32),
            pltpu.VMEM((NEWTON, column, 1, 128), f32),
            pltpu.VMEM((NEWTON, direct, 1, 128), f32),
            pltpu.VMEM((z, 1, 128), f32),
            pltpu.VMEM((column, 1, 128), f32),
            pltpu.VMEM((LEVELS, 1, 128), f32),
            pltpu.VMEM((plane, 1, 128), f32),
            pltpu.VMEM((direct, 1, 128), f32),
            pltpu.VMEM((1, 128), f32),
            pltpu.VMEM((1, 128), f32),
            pltpu.VMEM((1, 128), f32),
            pltpu.VMEM((1, 128), f32),
            pltpu.SemaphoreType.DMA((11,)),
            pltpu.SemaphoreType.DMA((NEWTON, 3)),
            pltpu.SemaphoreType.DMA((NEWTON, LEVELS + 2)),
            pltpu.SemaphoreType.DMA((3,)),
            pltpu.SemaphoreType.DMA((3,)),
            pltpu.SemaphoreType.DMA((3,)),
            pltpu.SemaphoreType.DMA((LEVELS + 2,)),
            pltpu.SemaphoreType.DMA((2,)),
            pltpu.SemaphoreType.DMA((2,)),
        ],
        compiler_params=pltpu.CompilerParams(
            collective_id=0, has_side_effects=True, vmem_limit_bytes=40 * 1024 * 1024
        ),
    )(
        in_hbm(taxa_states),
        in_hbm(outside.transpose(1, 0, 2)),
        in_hbm(children.T),
        in_hbm(branch),
        root_length.reshape(1, 1),
        in_hbm(cat_rates),
        in_hbm(exchange_rates),
        in_hbm(frequencies),
        in_hbm(pattern_idx.reshape(1, columns)),
        in_hbm(rivals),
        in_hbm(weights),
    )
    scores, loglik, root = pl.pallas_call(
        hand_over,
        out_shape=(
            jax.ShapeDtypeStruct((4, CAND), f32),
            jax.ShapeDtypeStruct((1, patterns), f32),
            jax.ShapeDtypeStruct((1, 128), f32),
        ),
        in_specs=[hbm] * 3,
        out_specs=(pl.BlockSpec(memory_space=pltpu.HBM),) * 3,
        scratch_shapes=[pltpu.SemaphoreType.DMA((3,))],
        compiler_params=pltpu.CompilerParams(vmem_limit_bytes=16 * 1024 * 1024),
    )(scores, loglik, root)
    return scores.T, loglik.reshape(patterns), root[0, 0:1]


def solution(mesh):
    placed = (
        P(None, ("cols", "rep")),
        P(None, None, ("cols", "rep")),
        P(),
        P(),
        P(),
        P(),
        P(),
        P(),
        P(None, ("cols", "rep")),
        P(("cols", "rep")),
        P(None, ("cols", "rep")),
    )
    return jax.shard_map(
        functools.partial(on_device, layout_of(mesh)),
        mesh=mesh,
        in_specs=placed,
        out_specs=(P(None, ("cols", "rep")), P(("cols", "rep")), P()),
        check_vma=False,
    )
```
